128 devices in a mesh: row: 8 (over x, core), col: 8 (over y, z_lo), chan: 2 (over z_hi).
Axes of the slice: x: 4, y: 4, z: 4 (z_hi: 2, z_lo: 2; z = z_hi * 2 + z_lo), core: 2. Of those that a mesh axis runs over, the one named last changes fastest.
Arguments:
- visibility: bfloat16 [8, 2, 64, 8, 8, 4096], P(None, None, 'chan', 'row', 'col'), may hold values from -6 to 6
- flags: int32 [2, 64, 8, 8, 4096], P(None, 'chan', 'row', 'col'), may hold values 0 or 1
- coeffs: float32 [512, 512], P(('row', 'col')), may hold values from -4 to 4
- station_uv: float32 [2, 2, 512], replicated, may hold values from -100 to 100
- source_lm: float32 [2, 256], replicated, may hold values from -0.1 to 0.1
- source_flux: float32 [256, 64], replicated, may hold values from 0.05 to 0.5
- cluster_ids: int32 [256], replicated, may hold values from 0 to 7
Outputs:
- coef_grad: float32 [512, 512], P(('row', 'col'))
The draws below stay inside these ranges and needn't reach their ends.
All inputs are finite; a program needn't handle non-finite values. No bound on the sum of `flags` on one device may be relied on, other than what follows from the above.
Results may differ from the reference program's by a relative error of at most 0.0003.
Values sent between devices are 32-bit elements; how exact they have to be, the bound alone decides.
No kernel may reach another device: no remote copies, remote signals or barrier semaphores. Data moves between devices by JAX's collectives and lax.ppermute only.
A program may use at most 128 MiB of HBM per device.

```python
import math
import jax
import jax.numpy as jnp
from jax import lax

S = 512
K = 8
F = 64
NB = 8
NSRC = 256
T_SMP = 2
CW = 512
NRB = 8
NCB = 8
RB = 64
CB = 64
BLK = 4096


def with_ends(drawn, key, smallest, largest):
    place = [jax.random.randint(jax.random.fold_in(key, axis), (), 0, length) for axis, length in enumerate(drawn.shape)]
    main_axis = drawn.shape.index(max(drawn.shape))
    next_to = place[:main_axis] + [(place[main_axis] + 1) % drawn.shape[main_axis]] + place[main_axis + 1:]
    return drawn.at[tuple(place)].set(smallest).at[tuple(next_to)].set(largest)


def shard_levels(stream_key, dims, pieces, smallest, high):
    def one(axis_at, shards_of):
        draws = jax.random.uniform(jax.random.fold_in(jax.random.fold_in(stream_key, 6), axis_at), (shards_of,), jnp.float32, smallest / len(pieces), high / len(pieces))
        return jnp.repeat(jnp.exp(draws), dims[axis_at] // shards_of).reshape((-1,) + (1,) * (len(dims) - axis_at - 1))

    factor_of = one(*pieces[0])
    for cut in pieces[1:]:
        factor_of = factor_of * one(*cut)
    return factor_of


def centred(own_key, shape, scale, limit, pieces=(), held_as=jnp.bfloat16):
    loudness = shard_levels(own_key, shape, pieces, -0.22, 0.18) if pieces else 1.0
    result = jax.random.normal(own_key, shape, jnp.float32) * scale * loudness
    return jnp.minimum(jnp.maximum(result, -limit), limit).astype(held_as)


def setup_inputs(seed: int = 0) -> dict:
    splits = jax.random.split(jax.random.key(seed), 8)
    visibility = centred(splits[0], (8, T_SMP, F, NRB, NCB, BLK), 1.0, 6.0, ((2, 2), (3, 8), (4, 8)))
    flags = with_ends((jax.random.randint(splits[1], (T_SMP, F, NRB, NCB, BLK), 0, 10) < 9).astype(jnp.int32), jax.random.fold_in(splits[1], 1), 0, 1)
    coeffs = centred(splits[2], (S, CW), 0.3, 4.0, ((0, 64),), jnp.float32)
    station_uv = jnp.clip(jax.random.uniform(splits[3], (2, T_SMP, S), jnp.float32, -100.0, 100.0), -100.0, 100.0)
    source_lm = jnp.clip(jax.random.uniform(splits[4], (2, NSRC), jnp.float32, -0.1, 0.1), -0.1, 0.1)
    source_flux = jnp.clip(jnp.exp(jax.random.uniform(splits[5], (NSRC, F), jnp.float32, math.log(0.05), math.log(0.5))), 0.05, 0.5)
    cluster_ids = with_ends(jax.random.randint(splits[6], (NSRC,), 0, K), jax.random.fold_in(splits[6], 1), 0, K - 1).astype(jnp.int32)
    return dict(visibility=visibility, flags=flags, coeffs=coeffs, station_uv=station_uv, source_lm=source_lm, source_flux=source_flux, cluster_ids=cluster_ids)


two_pi = 2.0 * math.pi
dof_nu = 2.0

def bernstein(channel_index, nbasis):
    position = (channel_index.astype(jnp.float32) + 0.5) / F
    power = jnp.arange(nbasis).astype(jnp.float32)
    binomial = jnp.array([math.comb(nbasis - 1, degree) for degree in range(nbasis)], jnp.float32)
    return binomial[None, :] * position[:, None] ** power[None, :] * (1.0 - position)[:, None] ** (nbasis - 1.0 - power)[None, :]

def frequency(channel_index):
    return 1.0 + 0.5 * (channel_index.astype(jnp.float32) + 0.5) / F

def geometry(station_uv, source_lm):
    return station_uv[0][:, :, None] * source_lm[0][None, None, :] + station_uv[1][:, :, None] * source_lm[1][None, None, :]

def coherency(geom_row, geom_col, freq, weights):
    phase_row = two_pi * freq * geom_row
    phase_col = two_pi * freq * geom_col
    cos_row = jnp.cos(phase_row)
    sin_row = jnp.sin(phase_row)
    cos_col = jnp.cos(phase_col)
    sin_col = jnp.sin(phase_col)
    left_cos = weights[None, :, None, :] * cos_row[:, None, :, :]
    left_sin = weights[None, :, None, :] * sin_row[:, None, :, :]
    right_one = jnp.concatenate([cos_col, sin_col], axis=2)
    right_two = jnp.concatenate([sin_col, cos_col], axis=2)
    real_part = jnp.einsum('tkps,tqs->tkpq', jnp.concatenate([left_cos, left_sin], axis=3), right_one, precision=lax.Precision.HIGHEST)
    imag_part = jnp.einsum('tkps,tqs->tkpq', jnp.concatenate([left_cos, -left_sin], axis=3), right_two, precision=lax.Precision.HIGHEST)
    return (real_part, imag_part)

def jones_matrix(basis_row, coef_block):
    terms = jnp.einsum('b,pkbe->ekp', basis_row, coef_block, precision=lax.Precision.HIGHEST)
    identity = jnp.array([1.0, 0.0, 0.0, 0.0, 0.0, 0.0, 1.0, 0.0], jnp.float32)
    return terms + identity[:, None, None]

def channel_cost(jones_row, jones_col, real_part, imag_part, observed, weight_mask, scale):
    squared = None
    for row_pol in range(2):
        for col_pol in range(2):
            prod_re = 0.0
            prod_im = 0.0
            for shared in range(2):
                left_re = jones_row[2 * (2 * row_pol + shared)][:, :, None]
                left_im = jones_row[2 * (2 * row_pol + shared) + 1][:, :, None]
                right_re = jones_col[2 * (2 * col_pol + shared)][:, None, :]
                right_im = jones_col[2 * (2 * col_pol + shared) + 1][:, None, :]
                prod_re = prod_re + left_re * right_re + left_im * right_im
                prod_im = prod_im + left_im * right_re - left_re * right_im
            model_re = lax.optimization_barrier(jnp.sum(real_part * prod_re[None] - imag_part * prod_im[None], axis=1))
            model_im = lax.optimization_barrier(jnp.sum(real_part * prod_im[None] + imag_part * prod_re[None], axis=1))
            component = 2 * (2 * row_pol + col_pol)
            resid_re = observed[component] - model_re
            resid_im = observed[component + 1] - model_im
            part = resid_re * resid_re + resid_im * resid_im
            squared = part if squared is None else squared + part
    robust = weight_mask * ((dof_nu + 8.0) / 2.0) * jnp.log1p(squared / dof_nu)
    return jnp.sum(robust) * scale

def channel_gradient(jones_row, jones_col, real_part, imag_part, observed, weight_mask, scale):

    def cost_of(first, second):
        return channel_cost(first, second, real_part, imag_part, observed, weight_mask, scale)
    value, pullback = jax.vjp(cost_of, jones_row, jones_col)
    return pullback(jnp.ones_like(value))

def reference(visibility, flags, coeffs, station_uv, source_lm, source_flux, cluster_ids):
    scale = 1.0 / math.sqrt(S * F * T_SMP)
    coef_all = coeffs.reshape(S, K, NB, 8)
    basis = bernstein(jnp.arange(F).astype(jnp.int32), NB)
    geom_all = geometry(station_uv, source_lm)
    onehot = (cluster_ids[None, :] == jnp.arange(K).astype(jnp.int32)[:, None]).astype(jnp.float32)

    def one_block(block):
        row_start = (block * RB).astype(jnp.int32)
        geom_row = lax.dynamic_slice_in_dim(geom_all, row_start, RB, 1)
        coef_row = lax.dynamic_slice_in_dim(coef_all, row_start, RB, 0)

        def one_channel(channel):
            basis_row = lax.dynamic_index_in_dim(basis, channel, 0, False)
            freq = frequency(channel)
            flux_now = lax.dynamic_index_in_dim(source_flux, channel, 1, False)
            real_part, imag_part = coherency(geom_row, geom_all, freq, onehot * flux_now[None, :])
            observed = lax.dynamic_index_in_dim(visibility, channel, 2, False)
            observed = lax.dynamic_index_in_dim(observed, block, 2, False)
            observed = observed.reshape(8, T_SMP, NCB, RB, CB).transpose(0, 1, 3, 2, 4).reshape(8, T_SMP, RB, S).astype(jnp.float32)
            weight_mask = lax.dynamic_index_in_dim(flags, channel, 1, False)
            weight_mask = lax.dynamic_index_in_dim(weight_mask, block, 1, False)
            weight_mask = weight_mask.reshape(T_SMP, NCB, RB, CB).transpose(0, 2, 1, 3).reshape(T_SMP, RB, S).astype(jnp.float32)
            jones_row = jones_matrix(basis_row, coef_row)
            jones_col = jones_matrix(basis_row, coef_all)
            return channel_gradient(jones_row, jones_col, real_part, imag_part, observed, weight_mask, scale)
        return lax.map(one_channel, jnp.arange(F).astype(jnp.int32))
    blocks = jnp.arange(NRB).astype(jnp.int32)
    grad_rows, grad_cols = lax.map(one_block, blocks)
    grad_rows = jnp.transpose(grad_rows, (1, 2, 3, 0, 4)).reshape(F, 8, K, S)
    grad_jones = grad_rows + lax.optimization_barrier(jnp.sum(grad_cols, axis=0))
    projected = jnp.einsum('fb,fekp->pkbe', basis, grad_jones, precision=lax.Precision.HIGHEST)
    return projected.reshape(S, K * NB * 8)
```

```python
import math

import jax
import jax.numpy as jnp
from jax import lax
from jax.experimental import pallas as pl
from jax.experimental.pallas import tpu as pltpu
from jax.sharding import PartitionSpec as P

S = 512
K = 8
F = 64
NB = 8
NSRC = 256
T_SMP = 2
RB = 64

f32 = jnp.float32
bf16 = jnp.bfloat16

SIN_TERMS = [(-1) ** n * math.pi ** (2 * n + 1) / math.factorial(2 * n + 1) for n in range(8)]
COS_TERMS = [(-1) ** n * math.pi ** (2 * n) / math.factorial(2 * n) for n in range(8)]


def bernstein(channel_index, nbasis):
    position = (channel_index.astype(f32) + 0.5) / F
    power = jnp.arange(nbasis).astype(f32)
    binomial = jnp.array([math.comb(nbasis - 1, degree) for degree in range(nbasis)], f32)
    return (
        binomial[None, :]
        * position[:, None] ** power[None, :]
        * (1.0 - position)[:, None] ** (nbasis - 1.0 - power)[None, :]
    )


def frequency(channel_index):
    return 1.0 + 0.5 * (channel_index.astype(f32) + 0.5) / F


def horner(terms, y):
    total = terms[-1]
    for term in terms[-2::-1]:
        total = total * y + term
    return total


def phasors(turns):
    r = turns - jnp.round(turns)
    y = r * r
    half_sin = r * horner(SIN_TERMS, y)
    half_cos = horner(COS_TERMS, y)
    return 1.0 - 2.0 * half_sin * half_sin, -2.0 * half_sin * half_cos


def split(x):
    high = x.astype(bf16)
    return high, (x - high.astype(f32)).astype(bf16)


def dot_nn(a, b):
    return lax.dot_general(a, b, (((1,), (0,)), ((), ())), preferred_element_type=f32)


def dot_nt(a, b):
    return lax.dot_general(a, b, (((1,), (1,)), ((), ())), preferred_element_type=f32)


def kernel(basis_ref, ids_ref, hot_ref, coef_ref, ec_ref, es_ref, vis_ref, flag_ref, out_ref,
           ct_ref, jg_ref, xh_ref, xl_ref, bh_ref, bl_ref, d_ref, acc_ref, turn_ref, pair_ref):
    step = pl.program_id(0)
    chans = pl.num_programs(0)
    odd = lax.broadcasted_iota(jnp.int32, (32, 128), 1) >= 64

    @pl.when(step == 0)
    def _():
        acc_ref[...] = jnp.zeros_like(acc_ref)
        for part in range(4):
            lanes = slice(part * 128, (part + 1) * 128)
            pair_ref[part] = coef_ref[0, :, lanes]
            ct_ref[lanes, :] = jnp.concatenate(
                [
                    pair_ref[part, pl.ds(0, 32, stride=2), :],
                    pair_ref[part, pl.ds(1, 32, stride=2), :],
                    coef_ref[1, :, lanes],
                ],
                axis=0,
            ).T

    element = lax.broadcasted_iota(jnp.int32, (8, 128), 0)
    identity = jnp.where((element == 0) | (element == 6), 1.0, 0.0).astype(f32)
    rows = []
    for k in range(K):
        total = identity
        for b in range(NB):
            total = total + basis_ref[step, b] * ct_ref[k * 64 + b * 8:k * 64 + b * 8 + 8, :]
        rows.append(total)
    jones = jnp.concatenate(rows + rows, axis=0).T
    halves = [jnp.broadcast_to(ids_ref[0:1, h * 128:(h + 1) * 128], (RB, 128)) for h in range(2)]
    for side in range(2):
        for e in range(8):
            for h in range(2):
                jg_ref[side, e, :, h * 128:(h + 1) * 128] = jnp.take_along_axis(
                    jones[side * RB:(side + 1) * RB], halves[h] + e, axis=1, mode="promise_in_bounds"
                )

    lane_row = step % 8
    for t in range(T_SMP):
        for side in range(2):
            er = ec_ref[0, t, side]
            ei = es_ref[0, t, side]
            high_ref, low_ref = (xh_ref, xl_ref) if side == 0 else (bh_ref, bl_ref)
            for i in range(2):
                for j in range(2):
                    jr = jg_ref[side, 2 * (2 * i + j)]
                    ji = jg_ref[side, 2 * (2 * i + j) + 1]
                    re = split(jr * er - ji * ei)
                    im = split(jr * ei + ji * er)
                    first = slice(i * RB, (i + 1) * RB)
                    second = slice(128 + i * RB, 128 + (i + 1) * RB)
                    left = slice(j * 256, (j + 1) * 256)
                    right = slice(512 + j * 256, 512 + (j + 1) * 256)
                    for ref, a, b in zip((high_ref, low_ref), re, im):
                        ref[t, first, left] = a
                        ref[t, first, right] = b
                        if side == 0:
                            ref[t, second, left] = b
                            ref[t, second, right] = -a
                        else:
                            ref[t, second, left] = -b
                            ref[t, second, right] = a
        x_high, x_low = xh_ref[t, 0:128], xl_ref[t, 0:128]
        b_high, b_low = bh_ref[t], bl_ref[t]
        model = dot_nt(x_high, b_high) + dot_nt(x_low, b_high) + dot_nt(x_high, b_low)
        observed = []
        for i in range(2):
            columns = []
            for c in range(2):
                one = vis_ref[4 * i + c, t, 0, pl.ds(lane_row, 32, stride=8), :]
                two = vis_ref[4 * i + 2 + c, t, 0, pl.ds(lane_row, 32, stride=8), :]
                columns.append((
                    jnp.where(odd, pltpu.roll(two, 64, 1), one),
                    jnp.where(odd, two, pltpu.roll(one, 64, 1)),
                ))
            observed.append(jnp.concatenate(
                [jnp.concatenate([columns[0][h], columns[1][h]], axis=1) for h in range(2)], axis=0
            ))
        resid = model - jnp.concatenate(observed, axis=0)
        square = resid * resid
        square = square[0:64] + square[64:128]
        square = square[:, 0:128] + square[:, 128:256]
        square = square + pltpu.roll(square, 64, 1)
        flag = flag_ref[t, 0].astype(f32)
        other = pltpu.roll(flag, 64, 1)
        flag = jnp.concatenate([jnp.where(odd, other, flag), jnp.where(odd, flag, other)], axis=0)
        weight = flag / (2.0 + square)
        weight = jnp.concatenate([weight, weight], axis=0)
        g_re = resid[:, 0:128] * weight
        g_im = resid[:, 128:256] * weight
        for side in range(2):
            if side == 0:
                g_high, g_low = split(jnp.concatenate([g_re, g_im], axis=1))
                m_high, m_low = bh_ref, bl_ref
            else:
                g_high, g_low = split(jnp.concatenate([g_re.T, g_im.T], axis=1))
                m_high, m_low = xh_ref, xl_ref
            er = ec_ref[0, t, side]
            ei = es_ref[0, t, side]
            for j in range(2):
                parts = []
                for c in range(2):
                    cols = slice(c * 512 + j * 256, c * 512 + (j + 1) * 256)
                    w_high = m_high[t, :, cols]
                    w_low = m_low[t, :, cols]
                    parts.append(dot_nn(g_high, w_high) + dot_nn(g_low, w_high) + dot_nn(g_high, w_low))
                for i in range(2):
                    dr = parts[0][i * RB:(i + 1) * RB]
                    di = parts[1][i * RB:(i + 1) * RB]
                    e = 2 * (2 * i + j)
                    jr = dr * er + di * ei
                    ji = di * er - dr * ei
                    if t == 0:
                        d_ref[side, e * RB:(e + 1) * RB] = jr
                        d_ref[side, (e + 1) * RB:(e + 2) * RB] = ji
                    else:
                        d_ref[side, e * RB:(e + 1) * RB] += jr
                        d_ref[side, (e + 1) * RB:(e + 2) * RB] += ji

    for side in range(2):
        d_high, d_low = split(d_ref[side])
        summed = (dot_nt(hot_ref[...], d_high) + dot_nt(hot_ref[...], d_low))[0:8]
        for b in range(NB):
            acc_ref[b, side] += basis_ref[step, b] * summed

    @pl.when(step == chans - 1)
    def _():
        for b in range(NB):
            for e in range(8):
                turn_ref[pl.ds(b * 8 + e, 8, stride=64), :] = jnp.concatenate(
                    [acc_ref[b, side, :, e * RB:(e + 1) * RB] for side in range(2)], axis=1
                )
        turned = turn_ref[...].T
        out_ref[1] = turned[64:128]
        for part in range(4):
            lanes = slice(part * 128, (part + 1) * 128)
            pair_ref[part, pl.ds(0, 32, stride=2), :] = turned[0:32, lanes]
            pair_ref[part, pl.ds(1, 32, stride=2), :] = turned[32:64, lanes]
            out_ref[0, :, lanes] = pair_ref[part]


def gradient_call(basis, ids, hot, coef, ec, es, vis, flag):
    chans = ec.shape[0]
    const = lambda shape: pl.BlockSpec(shape, lambda f: (0,) * len(shape))
    return pl.pallas_call(
        kernel,
        grid=(chans,),
        in_specs=[
            pl.BlockSpec(memory_space=pltpu.SMEM),
            const((8, NSRC)),
            const((16, NSRC)),
            const((2, RB, 512)),
            pl.BlockSpec((1, T_SMP, 2, RB, NSRC), lambda f: (f, 0, 0, 0, 0)),
            pl.BlockSpec((1, T_SMP, 2, RB, NSRC), lambda f: (f, 0, 0, 0, 0)),
            pl.BlockSpec((8, T_SMP, 1, 256, 128), lambda f: (0, 0, f // 8, 0, 0)),
            pl.BlockSpec((T_SMP, 1, 32, 128), lambda f: (0, f, 0, 0)),
        ],
        out_specs=const((2, RB, 512)),
        out_shape=jax.ShapeDtypeStruct((2, RB, 512), f32),
        scratch_shapes=[
            pltpu.VMEM((512, 128), f32),
            pltpu.VMEM((2, 8, RB, NSRC), f32),
            pltpu.VMEM((T_SMP, 256, 1024), bf16),
            pltpu.VMEM((T_SMP, 256, 1024), bf16),
            pltpu.VMEM((T_SMP, 256, 1024), bf16),
            pltpu.VMEM((T_SMP, 256, 1024), bf16),
            pltpu.VMEM((2, 512, NSRC), f32),
            pltpu.VMEM((NB, 2, K, 512), f32),
            pltpu.VMEM((512, 128), f32),
            pltpu.VMEM((4, RB, 128), f32),
        ],
        compiler_params=pltpu.CompilerParams(
            dimension_semantics=("arbitrary",), vmem_limit_bytes=40 * 1024 * 1024
        ),
        cost_estimate=pl.CostEstimate(
            flops=2 * 3 * 6 * 128 * 1024 * 256 * T_SMP * chans, bytes_accessed=24 * 1024 * 1024, transcendentals=0
        ),
        name="robust_gradient",
    )(basis, ids, hot, coef, ec, es, vis, flag)


CROSS = [(r * 8 + c, c * 8 + r) for r in range(8) for c in range(8)]


def gather_block(own):
    col = lax.axis_index("col")
    held = own
    for bit in (1, 2, 4):
        other = lax.ppermute(held, "col", [(c, c ^ bit) for c in range(8)])
        upper = (col & bit) != 0
        held = jnp.concatenate([jnp.where(upper, other, held), jnp.where(upper, held, other)], axis=0)
    return held


def per_device(visibility, flags, coeffs, station_uv, source_lm, source_flux, cluster_ids):
    scale = 1.0 / math.sqrt(S * F * T_SMP)
    chans = visibility.shape[2]
    row = lax.axis_index("row")
    col = lax.axis_index("col")
    chan_start = lax.axis_index("chan") * chans
    channels = chan_start + jnp.arange(chans)

    row_coef = gather_block(coeffs)
    col_coef = lax.ppermute(row_coef, ("row", "col"), CROSS)
    coef = jnp.stack([row_coef, col_coef])

    basis = bernstein(channels, NB)
    row_uv = lax.dynamic_slice_in_dim(station_uv, row * RB, RB, 2)
    row_uv = row_uv.reshape(2, T_SMP, 32, 2).transpose(0, 1, 3, 2).reshape(2, T_SMP, RB)
    col_uv = lax.dynamic_slice_in_dim(station_uv, col * RB, RB, 2)
    uv = jnp.stack([row_uv, col_uv], axis=2)
    geo = uv[0][..., None] * source_lm[0] + uv[1][..., None] * source_lm[1]
    turns = frequency(channels)[:, None, None, None, None] * geo[None]
    flux = lax.dynamic_slice_in_dim(source_flux, chan_start, chans, 1).T
    amplitude = jnp.stack([flux, jnp.ones_like(flux)], axis=1)[:, None, :, None, :]
    cosine, sine = phasors(turns)
    ids = jnp.broadcast_to(cluster_ids[None] * 8, (8, NSRC))
    hot = (cluster_ids[None] == jnp.arange(16)[:, None]).astype(bf16)

    vis = visibility.astype(f32).reshape(8, T_SMP, chans // 8, 8, 32, 128)
    vis = vis.transpose(0, 1, 2, 4, 3, 5).reshape(8, T_SMP, chans // 8, 256, 128)
    flag = flags.reshape(T_SMP, chans, 32, 128)

    grad = gradient_call(basis, ids, hot, coef, cosine * amplitude, sine * amplitude, vis, flag)
    row_part = grad[0].reshape(8, 8, 512)
    col_part = lax.ppermute(grad[1], ("row", "col"), CROSS).reshape(8, 8, 512)
    both = jnp.concatenate([row_part, col_part], axis=1)
    both = lax.all_to_all(both, "col", 0, 0, tiled=True)
    total = both.reshape(16, 8, 512).sum(0) * (10.0 * scale)
    return total + lax.ppermute(total, "chan", [(0, 1), (1, 0)])


def solution(mesh):
    return jax.shard_map(
        per_device,
        mesh=mesh,
        in_specs=(
            P(None, None, "chan", "row", "col", None),
            P(None, "chan", "row", "col", None),
            P(("row", "col"), None),
            P(),
            P(),
            P(),
            P(),
        ),
        out_specs=P(("row", "col"), None),
        check_vma=False,
    )
```

```python
import math

import jax
import jax.numpy as jnp
from jax import lax
from jax.experimental import pallas as pl
from jax.experimental.pallas import tpu as pltpu
from jax.sharding import PartitionSpec as P

S = 512
K = 8
F = 64
NB = 8
NSRC = 256
T_SMP = 2
RB = 64
SCALE = 10.0 / math.sqrt(S * F * T_SMP)

f32 = jnp.float32
bf16 = jnp.bfloat16

SIN_TERMS = [(-1) ** n * math.pi ** (2 * n + 1) / math.factorial(2 * n + 1) for n in range(8)]
COS_TERMS = [(-1) ** n * math.pi ** (2 * n) / math.factorial(2 * n) for n in range(8)]


def bernstein(channel_index, nbasis):
    position = (channel_index.astype(f32) + 0.5) / F
    power = jnp.arange(nbasis).astype(f32)
    binomial = jnp.array([math.comb(nbasis - 1, degree) for degree in range(nbasis)], f32)
    return (
        binomial[None, :]
        * position[:, None] ** power[None, :]
        * (1.0 - position)[:, None] ** (nbasis - 1.0 - power)[None, :]
    )


def frequency(channel_index):
    return 1.0 + 0.5 * (channel_index.astype(f32) + 0.5) / F


def horner(terms, y):
    total = terms[-1]
    for term in terms[-2::-1]:
        total = total * y + term
    return total


def phasors(turns):
    r = turns - jnp.round(turns)
    y = r * r
    half_sin = r * horner(SIN_TERMS, y)
    half_cos = horner(COS_TERMS, y)
    return 1.0 - 2.0 * half_sin * half_sin, -2.0 * half_sin * half_cos


def split(x):
    high = x.astype(bf16)
    return high, (x - high.astype(f32)).astype(bf16)


def dot_nn(a, b):
    return lax.dot_general(a, b, (((1,), (0,)), ((), ())), preferred_element_type=f32)


def dot_nt(a, b):
    return lax.dot_general(a, b, (((1,), (1,)), ((), ())), preferred_element_type=f32)


def product(a, b):
    return dot_nn(a[0], b[0]) + dot_nn(a[1], b[0]) + dot_nn(a[0], b[1])


def kernel(basis_ref, ids_ref, hot_ref, hott_ref, coef_ref, c0_ref, c1_ref, s0_ref, s1_ref, c0n_ref, c1n_ref, s0n_ref,
           s1n_ref, vis_ref, flag_ref, row_ref, col_ref, ct_ref, cq_ref, jn0_ref, jn1_ref, jt0_ref, jt1_ref, x0h, x0l, x1h, x1l,
           w0h, w0l, w1h, w1l, dp0_ref, dp1_ref, dq0_ref, dq1_ref, acc_ref, pair_ref):
    step = pl.program_id(0)
    now = ((c0_ref, c1_ref), (s0_ref, s1_ref))
    ahead = ((c0n_ref, c1n_ref), (s0n_ref, s1n_ref))
    steps = pl.num_programs(0)
    odd = lax.broadcasted_iota(jnp.int32, (32, 128), 1) >= 64
    x_refs = ((x0h, x0l), (x1h, x1l))
    w_refs = ((w0h, w0l), (w1h, w1l))
    jn_refs, jt_refs = (jn0_ref, jn1_ref), (jt0_ref, jt1_ref)
    dp_refs, dq_refs = (dp0_ref, dp1_ref), (dq0_ref, dq1_ref)

    def prepare(slot, chan, table, at):
        jn_ref, jt_ref = jn_refs[slot], jt_refs[slot]
        element = lax.broadcasted_iota(jnp.int32, (8, 128), 0)
        identity = jnp.where((element == 0) | (element == 6), 1.0, 0.0).astype(f32)
        rows = []
        for k in range(K):
            total = identity
            for b in range(NB):
                total = total + basis_ref[chan, b] * ct_ref[k * 64 + b * 8:k * 64 + b * 8 + 8, :]
            rows.append(total)
        jones = jnp.concatenate(rows + rows, axis=0).T[0:RB]
        halves = [jnp.broadcast_to(ids_ref[0:1, h * 128:(h + 1) * 128], (RB, 128)) for h in range(2)]
        for e in range(8):
            for h in range(2):
                jn_ref[e, :, h * 128:(h + 1) * 128] = jnp.take_along_axis(
                    jones, halves[h] + e, axis=1, mode="promise_in_bounds"
                )
        place = lax.broadcasted_iota(jnp.int32, (K, 512), 1)
        total = jnp.where((place < 64) | ((place >= 320) & (place < 384)), 1.0, 0.0).astype(f32)
        for b in range(NB):
            total = total + basis_ref[chan, b] * cq_ref[b]
        high, low = split(total)
        total = dot_nn(hott_ref[...], jnp.concatenate([high.astype(f32), low.astype(f32)], axis=0).astype(bf16))
        for part in range(4):
            jt_ref[part] = total[:, part * 128:(part + 1) * 128]
        for t in range(T_SMP):
            er, ei = table[0][t][at, 0], table[1][t][at, 0]
            for j in range(2):
                for i in range(2):
                    jr = jn_ref[4 * i + 2 * j]
                    ji = jn_ref[4 * i + 2 * j + 1]
                    for c, value in enumerate((jr * er - ji * ei, jr * ei + ji * er)):
                        spot = slice(c * 128 + i * RB, c * 128 + (i + 1) * RB)
                        for ref, part in zip(x_refs[slot], split(value)):
                            ref[t, spot, j * 256:(j + 1) * 256] = part
            er, ei = table[0][t][at, 1], table[1][t][at, 1]
            er = jnp.concatenate([er, er], axis=0).T
            ei = jnp.concatenate([ei, ei], axis=0).T
            for j in range(2):
                jr = jt_ref[2 * j]
                ji = jt_ref[2 * j + 1]
                for c, value in enumerate((jr * er - ji * ei, jr * ei + ji * er)):
                    for ref, part in zip(w_refs[slot], split(value)):
                        ref[t, j * 256:(j + 1) * 256, c * 128:(c + 1) * 128] = part

    def forward(slot, t, row):
        result = product([ref[t] for ref in x_refs[slot]], [ref[t] for ref in w_refs[slot]])
        model = (
            result[0:128, 0:128] + result[128:256, 128:256],
            result[128:256, 0:128] - result[0:128, 128:256],
        )
        resid = []
        for c in range(2):
            observed = []
            for i in range(2):
                one = vis_ref[4 * i + c, t, 0, pl.ds(row, 32, stride=8), :]
                two = vis_ref[4 * i + 2 + c, t, 0, pl.ds(row, 32, stride=8), :]
                observed.append(jnp.where(odd, pltpu.roll(two, 64, 1), one))
                observed.append(jnp.where(odd, two, pltpu.roll(one, 64, 1)))
            resid.append(model[c] - jnp.concatenate(observed, axis=0))
        square = resid[0] * resid[0] + resid[1] * resid[1]
        square = square[0:64] + square[64:128]
        square = square + pltpu.roll(square, 64, 1)
        flag = flag_ref[t, slot].astype(f32) * SCALE
        other = pltpu.roll(flag, 64, 1)
        flag = jnp.concatenate([jnp.where(odd, other, flag), jnp.where(odd, flag, other)], axis=0)
        weight = flag / (2.0 + square)
        weight = jnp.concatenate([weight, weight], axis=0)
        re = (resid[0] * weight).T
        im = (resid[1] * weight).T
        return split(
            jnp.concatenate([jnp.concatenate([re, im], axis=1), jnp.concatenate([-im, re], axis=1)], axis=0)
        )

    def backward(slot, t, g):
        dp_ref, dq_ref = dp_refs[slot], dq_refs[slot]
        er, ei = now[0][t][slot, 0], now[1][t][slot, 0]
        er = jnp.concatenate([er, er], axis=0).T
        ei = jnp.concatenate([ei, ei], axis=0).T
        for j in range(2):
            part = product([ref[t, j * 256:(j + 1) * 256] for ref in w_refs[slot]], g)
            dr, di = part[:, 0:128], part[:, 128:256]
            jr = dr * er + di * ei
            ji = di * er - dr * ei
            if t > 0:
                jr = jr + dp_ref[:, (2 * j) * 128:(2 * j + 1) * 128]
                ji = ji + dp_ref[:, (2 * j + 1) * 128:(2 * j + 2) * 128]
            dp_ref[:, (2 * j) * 128:(2 * j + 1) * 128] = jr
            dp_ref[:, (2 * j + 1) * 128:(2 * j + 2) * 128] = ji
        er, ei = now[0][t][slot, 1], now[1][t][slot, 1]
        for j in range(2):
            part = product(g, [ref[t, :, j * 256:(j + 1) * 256] for ref in x_refs[slot]])
            for i in range(2):
                dr, di = part[i * RB:(i + 1) * RB], part[128 + i * RB:128 + (i + 1) * RB]
                jr = dr * er + di * ei
                ji = di * er - dr * ei
                e = 4 * i + 2 * j
                if t > 0:
                    jr = jr + dq_ref[e * RB:(e + 1) * RB]
                    ji = ji + dq_ref[(e + 1) * RB:(e + 2) * RB]
                dq_ref[e * RB:(e + 1) * RB] = jr
                dq_ref[(e + 1) * RB:(e + 2) * RB] = ji

    def collect(slot, chan):
        hot = hot_ref[...]
        high, low = split(dp_refs[slot][...])
        sums = [(dot_nn(hot, high) + dot_nn(hot, low))[0:8]]
        high, low = split(dq_refs[slot][...])
        sums.append((dot_nt(hot, high) + dot_nt(hot, low))[0:8])
        for side in range(2):
            for b in range(NB):
                acc_ref[b, side] += basis_ref[chan, b] * sums[side]

    @pl.when(step == 0)
    def _():
        acc_ref[...] = jnp.zeros_like(acc_ref)
        for part in range(4):
            lanes = slice(part * 128, (part + 1) * 128)
            pair_ref[part] = coef_ref[0, :, lanes]
            ct_ref[lanes, :] = jnp.concatenate(
                [
                    pair_ref[part, pl.ds(0, 32, stride=2), :],
                    pair_ref[part, pl.ds(1, 32, stride=2), :],
                    coef_ref[1, :, lanes],
                ],
                axis=0,
            ).T
        for b in range(NB):
            for j in range(2):
                for c in range(2):
                    both = [ct_ref[pl.ds(b * 8 + 4 * i + 2 * j + c, 8, stride=64), :][:, 64:128] for i in range(2)]
                    cq_ref[b, :, (2 * j + c) * 128:(2 * j + c + 1) * 128] = jnp.concatenate(both, axis=1)
        prepare(0, 0, now, 0)

    first = 2 * step
    row = first % 8
    g = [forward(0, t, row) for t in range(T_SMP)]
    prepare(1, first + 1, now, 1)
    for t in range(T_SMP):
        backward(0, t, g[t])
    g = [forward(1, t, row + 1) for t in range(T_SMP)]
    prepare(0, jnp.minimum(first + 2, 2 * steps - 1), ahead, 0)
    collect(0, first)
    for t in range(T_SMP):
        backward(1, t, g[t])
    collect(1, first + 1)

    @pl.when(step == steps - 1)
    def _():
        for b in range(NB):
            for e in range(8):
                i, j, c = e // 4, e // 2 % 2, e % 2
                first = (4 * j + 2 * c + i) * RB
                ct_ref[pl.ds(b * 8 + e, 8, stride=64), :] = jnp.concatenate(
                    [acc_ref[b, 0, :, first:first + RB], acc_ref[b, 1, :, e * RB:(e + 1) * RB]], axis=1
                )
        turned = ct_ref[...].T
        col_ref[...] = turned[64:128]
        for part in range(4):
            lanes = slice(part * 128, (part + 1) * 128)
            pair_ref[part, pl.ds(0, 32, stride=2), :] = turned[0:32, lanes]
            pair_ref[part, pl.ds(1, 32, stride=2), :] = turned[32:64, lanes]
            row_ref[:, lanes] = pair_ref[part]


def gradient_call(basis, ids, hot, coef, cosines, sines, vis, flag):
    chans = basis.shape[0]
    const = lambda shape: pl.BlockSpec(shape, lambda f: (0,) * len(shape))
    hott = jnp.concatenate([hot[0:8], hot[0:8]], axis=0).T
    now = pl.BlockSpec((2, 2, RB, NSRC), lambda f: (f, 0, 0, 0))
    ahead = pl.BlockSpec((1, 2, RB, NSRC), lambda f: (jnp.minimum(2 * f + 2, chans - 1), 0, 0, 0))
    factors = []
    for shape in ((T_SMP, 256, 512), (T_SMP, 512, 256)):
        factors += [pltpu.VMEM(shape, bf16)] * 4
    return pl.pallas_call(
        kernel,
        grid=(chans // 2,),
        in_specs=[
            pl.BlockSpec(memory_space=pltpu.SMEM),
            const((8, NSRC)),
            const((16, NSRC)),
            const((NSRC, 16)),
            const((2, RB, 512)),
            *[now] * 4,
            *[ahead] * 4,
            pl.BlockSpec((8, T_SMP, 1, 256, 128), lambda f: (0, 0, f // 4, 0, 0)),
            pl.BlockSpec((T_SMP, 2, 32, 128), lambda f: (0, f, 0, 0)),
        ],
        out_specs=[const((RB, 512))] * 2,
        out_shape=[jax.ShapeDtypeStruct((RB, 512), f32)] * 2,
        scratch_shapes=[
            pltpu.VMEM((512, 128), f32),
            pltpu.VMEM((NB, K, 512), f32),
            pltpu.VMEM((8, RB, NSRC), f32),
            pltpu.VMEM((8, RB, NSRC), f32),
            pltpu.VMEM((4, NSRC, 128), f32),
            pltpu.VMEM((4, NSRC, 128), f32),
            *factors,
            pltpu.VMEM((NSRC, 512), f32),
            pltpu.VMEM((NSRC, 512), f32),
            pltpu.VMEM((512, NSRC), f32),
            pltpu.VMEM((512, NSRC), f32),
            pltpu.VMEM((NB, 2, K, 512), f32),
            pltpu.VMEM((4, RB, 128), f32),
        ],
        compiler_params=pltpu.CompilerParams(
            dimension_semantics=("arbitrary",), vmem_limit_bytes=60 * 1024 * 1024
        ),
        cost_estimate=pl.CostEstimate(
            flops=2 * 3 * 6 * 128 * 1024 * 256 * T_SMP * chans, bytes_accessed=24 * 1024 * 1024, transcendentals=0
        ),
        name="robust_gradient",
    )(basis, ids, hot, hott, coef, *cosines, *sines, *cosines, *sines, vis, flag)


CROSS = [(r * 8 + c, c * 8 + r) for r in range(8) for c in range(8)]


def merge(held, other, axis, bit):
    upper = (lax.axis_index(axis) & bit) != 0
    return jnp.concatenate([jnp.where(upper, other, held), jnp.where(upper, held, other)], axis=0)


def table(uv, source_lm, freq, amplitude):
    geo = uv[0][..., None] * source_lm[0] + uv[1][..., None] * source_lm[1]
    cosine, sine = phasors(freq[:, None, None, None] * geo[None])
    return cosine * amplitude, sine * amplitude


def per_device(visibility, flags, coeffs, station_uv, source_lm, source_flux, cluster_ids):
    chans = visibility.shape[2]
    row = lax.axis_index("row")
    col = lax.axis_index("col")
    chan_start = lax.axis_index("chan") * chans
    channels = chan_start + jnp.arange(chans)

    basis = bernstein(channels, NB)
    row_uv = lax.dynamic_slice_in_dim(station_uv, row * RB, RB, 2)
    row_uv = row_uv.reshape(2, T_SMP, 32, 2).transpose(0, 1, 3, 2).reshape(2, T_SMP, RB)
    col_uv = lax.dynamic_slice_in_dim(station_uv, col * RB, RB, 2)
    uv = jnp.stack([row_uv, col_uv], axis=2)
    freq = frequency(channels)
    flux = lax.dynamic_slice_in_dim(source_flux, chan_start, chans, 1).T
    amplitude = jnp.stack([flux, jnp.ones_like(flux)], axis=1)[:, :, None, :]
    ids = jnp.broadcast_to(cluster_ids[None] * 8, (8, NSRC))
    hot = (cluster_ids[None] == jnp.arange(16)[:, None]).astype(bf16)

    vis = visibility.astype(f32).reshape(8, T_SMP, chans // 8, 8, 32, 128)
    vis = vis.transpose(0, 1, 2, 4, 3, 5).reshape(8, T_SMP, chans // 8, 256, 128)
    flag = flags.reshape(T_SMP, chans, 32, 128)

    row_coef, col_coef = coeffs, None
    tables = []
    for bit, t in ((1, None), (2, 0), (4, 1)):
        if t is not None:
            uv_now = lax.optimization_barrier((uv[:, t], row_coef, col_coef, tables))[0]
        other = lax.ppermute(row_coef, "col", [(c, c ^ bit) for c in range(8)])
        if col_coef is None:
            col_coef = lax.ppermute(coeffs, ("row", "col"), CROSS)
        else:
            passed = lax.ppermute(col_coef, "row", [(r, r ^ (bit // 2)) for r in range(8)])
            col_coef = merge(col_coef, passed, "row", bit // 2)
        row_coef = merge(row_coef, other, "col", bit)
        if t is not None:
            tables.append(table(uv_now, source_lm, freq, amplitude))
    passed = lax.ppermute(col_coef, "row", [(r, r ^ 4) for r in range(8)])
    col_coef = merge(col_coef, passed, "row", 4)
    coef = jnp.stack([row_coef, col_coef])

    row_part, col_part = gradient_call(
        basis, ids, hot, coef, [t[0] for t in tables], [t[1] for t in tables], vis, flag
    )
    col_part = lax.ppermute(col_part, ("row", "col"), CROSS)
    both = jnp.concatenate([row_part.reshape(8, 8, 512), col_part.reshape(8, 8, 512)], axis=1)
    both = lax.all_to_all(both, "col", 0, 0, tiled=True)
    total = both.reshape(16, 8, 512).sum(0)
    return total + lax.ppermute(total, "chan", [(0, 1), (1, 0)])


def solution(mesh):
    return jax.shard_map(
        per_device,
        mesh=mesh,
        in_specs=(
            P(None, None, "chan", "row", "col", None),
            P(None, "chan", "row", "col", None),
            P(("row", "col"), None),
            P(),
            P(),
            P(),
            P(),
        ),
        out_specs=P(("row", "col"), None),
        check_vma=False,
    )
```

```python
import math

import jax
import jax.numpy as jnp
from jax import lax
from jax.experimental import pallas as pl
from jax.experimental.pallas import tpu as pltpu
from jax.sharding import PartitionSpec as P

S = 512
K = 8
F = 64
NB = 8
NSRC = 256
T_SMP = 2
RB = 64
SCALE = 10.0 / math.sqrt(S * F * T_SMP)

f32 = jnp.float32
bf16 = jnp.bfloat16

SIN_TERMS = [(-1) ** n * math.pi ** (2 * n + 1) / math.factorial(2 * n + 1) for n in range(8)]
COS_TERMS = [(-1) ** n * math.pi ** (2 * n) / math.factorial(2 * n) for n in range(8)]


def bernstein(channel_index, nbasis):
    position = (channel_index.astype(f32) + 0.5) / F
    power = jnp.arange(nbasis).astype(f32)
    binomial = jnp.array([math.comb(nbasis - 1, degree) for degree in range(nbasis)], f32)
    return (
        binomial[None, :]
        * position[:, None] ** power[None, :]
        * (1.0 - position)[:, None] ** (nbasis - 1.0 - power)[None, :]
    )


def frequency(channel_index):
    return 1.0 + 0.5 * (channel_index.astype(f32) + 0.5) / F


def horner(terms, y):
    total = terms[-1]
    for term in terms[-2::-1]:
        total = total * y + term
    return total


def phasors(turns):
    r = turns - jnp.round(turns)
    y = r * r
    half_sin = r * horner(SIN_TERMS, y)
    half_cos = horner(COS_TERMS, y)
    return 1.0 - 2.0 * half_sin * half_sin, -2.0 * half_sin * half_cos


def split(x):
    high = x.astype(bf16)
    return high, (x - high.astype(f32)).astype(bf16)


def dot_nn(a, b):
    return lax.dot_general(a, b, (((1,), (0,)), ((), ())), preferred_element_type=f32)


def dot_nt(a, b):
    return lax.dot_general(a, b, (((1,), (1,)), ((), ())), preferred_element_type=f32)


def product(a, b):
    return dot_nn(a[0], b[0]) + dot_nn(a[1], b[0]) + dot_nn(a[0], b[1])


def kernel(basis_ref, ids_ref, hot_ref, hott_ref, coef_ref, flux_ref, begin_ref, turn_ref, vis_ref, flag_ref, row_ref, col_ref, ct_ref, cq_ref, jn0_ref, jn1_ref, jt0_ref, jt1_ref, x0h, x0l, x1h, x1l,
           w0h, w0l, w1h, w1l, dp0_ref, dp1_ref, dq0_ref, dq1_ref, acc_ref, pair_ref,
           e0_ref, e1_ref, f0_ref, f1_ref):
    step = pl.program_id(0)
    e_refs, f_refs = (e0_ref, e1_ref), (f0_ref, f1_ref)
    steps = pl.num_programs(0)
    odd = lax.broadcasted_iota(jnp.int32, (32, 128), 1) >= 64
    x_refs = ((x0h, x0l), (x1h, x1l))
    w_refs = ((w0h, w0l), (w1h, w1l))
    jn_refs, jt_refs = (jn0_ref, jn1_ref), (jt0_ref, jt1_ref)
    dp_refs, dq_refs = (dp0_ref, dp1_ref), (dq0_ref, dq1_ref)

    def prepare(slot, chan, before):
        jn_ref, jt_ref = jn_refs[slot], jt_refs[slot]
        element = lax.broadcasted_iota(jnp.int32, (8, 128), 0)
        identity = jnp.where((element == 0) | (element == 6), 1.0, 0.0).astype(f32)
        rows = []
        for k in range(K):
            total = identity
            for b in range(NB):
                total = total + basis_ref[chan, b] * ct_ref[k * 64 + b * 8:k * 64 + b * 8 + 8, :]
            rows.append(total)
        jones = jnp.concatenate(rows + rows, axis=0).T[0:RB]
        halves = [jnp.broadcast_to(ids_ref[0:1, h * 128:(h + 1) * 128], (RB, 128)) for h in range(2)]
        for e in range(8):
            for h in range(2):
                jn_ref[e, :, h * 128:(h + 1) * 128] = jnp.take_along_axis(
                    jones, halves[h] + e, axis=1, mode="promise_in_bounds"
                )
        place = lax.broadcasted_iota(jnp.int32, (K, 512), 1)
        total = jnp.where((place < 64) | ((place >= 320) & (place < 384)), 1.0, 0.0).astype(f32)
        for b in range(NB):
            total = total + basis_ref[chan, b] * cq_ref[b]
        high, low = split(total)
        total = dot_nn(hott_ref[...], jnp.concatenate([high.astype(f32), low.astype(f32)], axis=0).astype(bf16))
        for part in range(4):
            jt_ref[part] = total[:, part * 128:(part + 1) * 128]
        for t in range(T_SMP):
            for side in range(2):
                er, ei = before[0, t, side], before[1, t, side]
                if before is not begin_ref:
                    sr, si = turn_ref[0, t, side], turn_ref[1, t, side]
                    er, ei = er * sr - ei * si, er * si + ei * sr
                e_refs[slot][0, t, side] = er
                e_refs[slot][1, t, side] = ei
            flux = flux_ref[pl.ds(chan, 1), :]
            er, ei = e_refs[slot][0, t, 0] * flux, e_refs[slot][1, t, 0] * flux
            f_refs[slot][0, t] = er
            f_refs[slot][1, t] = ei
            for j in range(2):
                for i in range(2):
                    jr = jn_ref[4 * i + 2 * j]
                    ji = jn_ref[4 * i + 2 * j + 1]
                    for c, value in enumerate((jr * er - ji * ei, jr * ei + ji * er)):
                        spot = slice(c * 128 + i * RB, c * 128 + (i + 1) * RB)
                        for ref, part in zip(x_refs[slot], split(value)):
                            ref[t, spot, j * 256:(j + 1) * 256] = part
            er, ei = e_refs[slot][0, t, 1], e_refs[slot][1, t, 1]
            er = jnp.concatenate([er, er], axis=0).T
            ei = jnp.concatenate([ei, ei], axis=0).T
            for j in range(2):
                jr = jt_ref[2 * j]
                ji = jt_ref[2 * j + 1]
                for c, value in enumerate((jr * er - ji * ei, jr * ei + ji * er)):
                    for ref, part in zip(w_refs[slot], split(value)):
                        ref[t, j * 256:(j + 1) * 256, c * 128:(c + 1) * 128] = part

    def forward(slot, t, row):
        result = product([ref[t] for ref in x_refs[slot]], [ref[t] for ref in w_refs[slot]])
        model = (
            result[0:128, 0:128] + result[128:256, 128:256],
            result[128:256, 0:128] - result[0:128, 128:256],
        )
        resid = []
        for c in range(2):
            observed = []
            for i in range(2):
                one = vis_ref[4 * i + c, t, 0, pl.ds(row, 32, stride=8), :]
                two = vis_ref[4 * i + 2 + c, t, 0, pl.ds(row, 32, stride=8), :]
                observed.append(jnp.where(odd, pltpu.roll(two, 64, 1), one))
                observed.append(jnp.where(odd, two, pltpu.roll(one, 64, 1)))
            resid.append(model[c] - jnp.concatenate(observed, axis=0))
        square = resid[0] * resid[0] + resid[1] * resid[1]
        square = square[0:64] + square[64:128]
        square = square + pltpu.roll(square, 64, 1)
        flag = flag_ref[t, slot].astype(f32) * SCALE
        other = pltpu.roll(flag, 64, 1)
        flag = jnp.concatenate([jnp.where(odd, other, flag), jnp.where(odd, flag, other)], axis=0)
        weight = flag / (2.0 + square)
        weight = jnp.concatenate([weight, weight], axis=0)
        re = (resid[0] * weight).T
        im = (resid[1] * weight).T
        return split(
            jnp.concatenate([jnp.concatenate([re, im], axis=1), jnp.concatenate([-im, re], axis=1)], axis=0)
        )

    def backward(slot, t, g):
        dp_ref, dq_ref = dp_refs[slot], dq_refs[slot]
        er, ei = f_refs[slot][0, t], f_refs[slot][1, t]
        er = jnp.concatenate([er, er], axis=0).T
        ei = jnp.concatenate([ei, ei], axis=0).T
        for j in range(2):
            part = product([ref[t, j * 256:(j + 1) * 256] for ref in w_refs[slot]], g)
            dr, di = part[:, 0:128], part[:, 128:256]
            jr = dr * er + di * ei
            ji = di * er - dr * ei
            if t > 0:
                jr = jr + dp_ref[:, (2 * j) * 128:(2 * j + 1) * 128]
                ji = ji + dp_ref[:, (2 * j + 1) * 128:(2 * j + 2) * 128]
            dp_ref[:, (2 * j) * 128:(2 * j + 1) * 128] = jr
            dp_ref[:, (2 * j + 1) * 128:(2 * j + 2) * 128] = ji
        er, ei = e_refs[slot][0, t, 1], e_refs[slot][1, t, 1]
        for j in range(2):
            part = product(g, [ref[t, :, j * 256:(j + 1) * 256] for ref in x_refs[slot]])
            for i in range(2):
                dr, di = part[i * RB:(i + 1) * RB], part[128 + i * RB:128 + (i + 1) * RB]
                jr = dr * er + di * ei
                ji = di * er - dr * ei
                e = 4 * i + 2 * j
                if t > 0:
                    jr = jr + dq_ref[e * RB:(e + 1) * RB]
                    ji = ji + dq_ref[(e + 1) * RB:(e + 2) * RB]
                dq_ref[e * RB:(e + 1) * RB] = jr
                dq_ref[(e + 1) * RB:(e + 2) * RB] = ji

    def collect(slot, chan):
        hot = hot_ref[...]
        high, low = split(dp_refs[slot][...])
        sums = [(dot_nn(hot, high) + dot_nn(hot, low))[0:8]]
        high, low = split(dq_refs[slot][...])
        sums.append((dot_nt(hot, high) + dot_nt(hot, low))[0:8])
        for side in range(2):
            for b in range(NB):
                acc_ref[b, side] += basis_ref[chan, b] * sums[side]

    @pl.when(step == 0)
    def _():
        acc_ref[...] = jnp.zeros_like(acc_ref)
        for part in range(4):
            lanes = slice(part * 128, (part + 1) * 128)
            pair_ref[part] = coef_ref[0, :, lanes]
            ct_ref[lanes, :] = jnp.concatenate(
                [
                    pair_ref[part, pl.ds(0, 32, stride=2), :],
                    pair_ref[part, pl.ds(1, 32, stride=2), :],
                    coef_ref[1, :, lanes],
                ],
                axis=0,
            ).T
        for b in range(NB):
            for j in range(2):
                for c in range(2):
                    both = [ct_ref[pl.ds(b * 8 + 4 * i + 2 * j + c, 8, stride=64), :][:, 64:128] for i in range(2)]
                    cq_ref[b, :, (2 * j + c) * 128:(2 * j + c + 1) * 128] = jnp.concatenate(both, axis=1)
        prepare(0, 0, begin_ref)

    first = 2 * step
    row = first % 8
    g = [forward(0, t, row) for t in range(T_SMP)]
    prepare(1, first + 1, e0_ref)
    for t in range(T_SMP):
        backward(0, t, g[t])
    g = [forward(1, t, row + 1) for t in range(T_SMP)]
    prepare(0, jnp.minimum(first + 2, 2 * steps - 1), e1_ref)
    collect(0, first)
    for t in range(T_SMP):
        backward(1, t, g[t])
    collect(1, first + 1)

    @pl.when(step == steps - 1)
    def _():
        for b in range(NB):
            for e in range(8):
                i, j, c = e // 4, e // 2 % 2, e % 2
                first = (4 * j + 2 * c + i) * RB
                ct_ref[pl.ds(b * 8 + e, 8, stride=64), :] = jnp.concatenate(
                    [acc_ref[b, 0, :, first:first + RB], acc_ref[b, 1, :, e * RB:(e + 1) * RB]], axis=1
                )
        turned = ct_ref[...].T
        col_ref[...] = turned[64:128]
        for part in range(4):
            lanes = slice(part * 128, (part + 1) * 128)
            pair_ref[part, pl.ds(0, 32, stride=2), :] = turned[0:32, lanes]
            pair_ref[part, pl.ds(1, 32, stride=2), :] = turned[32:64, lanes]
            row_ref[:, lanes] = pair_ref[part]


def gradient_call(basis, ids, hot, coef, flux, begin, turn, vis, flag):
    chans = basis.shape[0]
    const = lambda shape: pl.BlockSpec(shape, lambda f: (0,) * len(shape))
    hott = jnp.concatenate([hot[0:8], hot[0:8]], axis=0).T
    factors = []
    for shape in ((T_SMP, 256, 512), (T_SMP, 512, 256)):
        factors += [pltpu.VMEM(shape, bf16)] * 4
    return pl.pallas_call(
        kernel,
        grid=(chans // 2,),
        in_specs=[
            pl.BlockSpec(memory_space=pltpu.SMEM),
            const((8, NSRC)),
            const((16, NSRC)),
            const((NSRC, 16)),
            const((2, RB, 512)),
            const(flux.shape),
            const(begin.shape),
            const(turn.shape),
            pl.BlockSpec((8, T_SMP, 1, 256, 128), lambda f: (0, 0, f // 4, 0, 0)),
            pl.BlockSpec((T_SMP, 2, 32, 128), lambda f: (0, f, 0, 0)),
        ],
        out_specs=[const((RB, 512))] * 2,
        out_shape=[jax.ShapeDtypeStruct((RB, 512), f32)] * 2,
        scratch_shapes=[
            pltpu.VMEM((512, 128), f32),
            pltpu.VMEM((NB, K, 512), f32),
            pltpu.VMEM((8, RB, NSRC), f32),
            pltpu.VMEM((8, RB, NSRC), f32),
            pltpu.VMEM((4, NSRC, 128), f32),
            pltpu.VMEM((4, NSRC, 128), f32),
            *factors,
            pltpu.VMEM((NSRC, 512), f32),
            pltpu.VMEM((NSRC, 512), f32),
            pltpu.VMEM((512, NSRC), f32),
            pltpu.VMEM((512, NSRC), f32),
            pltpu.VMEM((NB, 2, K, 512), f32),
            pltpu.VMEM((4, RB, 128), f32),
            *[pltpu.VMEM((2, T_SMP, 2, RB, NSRC), f32)] * 2,
            *[pltpu.VMEM((2, T_SMP, RB, NSRC), f32)] * 2,
        ],
        compiler_params=pltpu.CompilerParams(
            dimension_semantics=("arbitrary",), vmem_limit_bytes=60 * 1024 * 1024
        ),
        cost_estimate=pl.CostEstimate(
            flops=2 * 3 * 6 * 128 * 1024 * 256 * T_SMP * chans, bytes_accessed=24 * 1024 * 1024, transcendentals=0
        ),
        name="robust_gradient",
    )(basis, ids, hot, hott, coef, flux, begin, turn, vis, flag)


CROSS = [(r * 8 + c, c * 8 + r) for r in range(8) for c in range(8)]


def merge(held, other, axis, bit):
    upper = (lax.axis_index(axis) & bit) != 0
    return jnp.concatenate([jnp.where(upper, other, held), jnp.where(upper, held, other)], axis=0)


def scatter(held, axis):
    size = lax.axis_size(axis)
    for bit in (4, 2, 1):
        half = held.shape[0] // 2
        upper = (lax.axis_index(axis) & bit) != 0
        low, high = held[:half], held[half:]
        passed = lax.ppermute(jnp.where(upper, low, high), axis, [(r, r ^ bit) for r in range(size)])
        held = jnp.where(upper, high, low) + passed
    return held


def per_device(visibility, flags, coeffs, station_uv, source_lm, source_flux, cluster_ids):
    chans = visibility.shape[2]
    row = lax.axis_index("row")
    col = lax.axis_index("col")
    chan_start = lax.axis_index("chan") * chans
    channels = chan_start + jnp.arange(chans)

    basis = bernstein(channels, NB)
    row_uv = lax.dynamic_slice_in_dim(station_uv, row * RB, RB, 2)
    row_uv = row_uv.reshape(2, T_SMP, 32, 2).transpose(0, 1, 3, 2).reshape(2, T_SMP, RB)
    col_uv = lax.dynamic_slice_in_dim(station_uv, col * RB, RB, 2)
    uv = jnp.stack([row_uv, col_uv], axis=2)
    geo = uv[0][..., None] * source_lm[0] + uv[1][..., None] * source_lm[1]
    begin = jnp.stack(phasors(frequency(chan_start) * geo))
    turn = jnp.stack(phasors((0.5 / F) * geo))
    flux = lax.dynamic_slice_in_dim(source_flux, chan_start, chans, 1).T
    ids = jnp.broadcast_to(cluster_ids[None] * 8, (8, NSRC))
    hot = (cluster_ids[None] == jnp.arange(16)[:, None]).astype(bf16)

    vis = visibility.astype(f32).reshape(8, T_SMP, chans // 8, 8, 32, 128)
    vis = vis.transpose(0, 1, 2, 4, 3, 5).reshape(8, T_SMP, chans // 8, 256, 128)
    flag = flags.reshape(T_SMP, chans, 32, 128)

    row_coef = coeffs
    col_coef = lax.ppermute(coeffs, ("row", "col"), CROSS)
    for bit in (1, 2, 4):
        row_coef = merge(row_coef, lax.ppermute(row_coef, "col", [(c, c ^ bit) for c in range(8)]), "col", bit)
        col_coef = merge(col_coef, lax.ppermute(col_coef, "row", [(r, r ^ bit) for r in range(8)]), "row", bit)
    coef = jnp.stack([row_coef, col_coef])

    row_part, col_part = gradient_call(basis, ids, hot, coef, flux, begin, turn, vis, flag)
    row_sum, col_sum = scatter(row_part, "col"), scatter(col_part, "row")
    axes = ("row", "col", "chan")
    swapped = [((r * 8 + c) * 2 + h, (r * 8 + c) * 2 + 1 - h) for r in range(8) for c in range(8) for h in range(2)]
    crossed = [((r * 8 + c) * 2 + h, (c * 8 + r) * 2 + h) for r in range(8) for c in range(8) for h in range(2)]
    both = [((r * 8 + c) * 2 + h, (c * 8 + r) * 2 + 1 - h) for r in range(8) for c in range(8) for h in range(2)]
    rows = row_sum + lax.ppermute(row_sum, axes, swapped)
    return rows + (lax.ppermute(col_sum, axes, crossed) + lax.ppermute(col_sum, axes, both))


def solution(mesh):
    return jax.shard_map(
        per_device,
        mesh=mesh,
        in_specs=(
            P(None, None, "chan", "row", "col", None),
            P(None, "chan", "row", "col", None),
            P(("row", "col"), None),
            P(),
            P(),
            P(),
            P(),
        ),
        out_specs=P(("row", "col"), None),
        check_vma=False,
    )
```

```python
import math

import jax
import jax.numpy as jnp
from jax import lax
from jax.experimental import pallas as pl
from jax.experimental.pallas import tpu as pltpu
from jax.sharding import PartitionSpec as P

S = 512
K = 8
F = 64
NB = 8
NSRC = 256
T_SMP = 2
RB = 64
BLK = 4096
SCALE = 10.0 / math.sqrt(S * F * T_SMP)

f32 = jnp.float32
bf16 = jnp.bfloat16

SIN_TERMS = [(-1) ** n * math.pi ** (2 * n + 1) / math.factorial(2 * n + 1) for n in range(8)]
COS_TERMS = [(-1) ** n * math.pi ** (2 * n) / math.factorial(2 * n) for n in range(8)]


def bernstein(channel_index, nbasis):
    position = (channel_index.astype(f32) + 0.5) / F
    power = jnp.arange(nbasis).astype(f32)
    binomial = jnp.array([math.comb(nbasis - 1, degree) for degree in range(nbasis)], f32)
    return (
        binomial[None, :]
        * position[:, None] ** power[None, :]
        * (1.0 - position)[:, None] ** (nbasis - 1.0 - power)[None, :]
    )


def frequency(channel_index):
    return 1.0 + 0.5 * (channel_index.astype(f32) + 0.5) / F


def horner(terms, y):
    total = terms[-1]
    for term in terms[-2::-1]:
        total = total * y + term
    return total


def phasors(turns):
    r = turns - jnp.round(turns)
    y = r * r
    half_sin = r * horner(SIN_TERMS, y)
    half_cos = horner(COS_TERMS, y)
    return 1.0 - 2.0 * half_sin * half_sin, -2.0 * half_sin * half_cos


def split(x):
    high = x.astype(bf16)
    return high, (x - high.astype(f32)).astype(bf16)


def dot_nn(a, b):
    return lax.dot_general(a, b, (((1,), (0,)), ((), ())), preferred_element_type=f32)


def dot_nt(a, b):
    return lax.dot_general(a, b, (((1,), (1,)), ((), ())), preferred_element_type=f32)


def product(a, b):
    return dot_nn(a[0], b[0]) + dot_nn(a[1], b[0]) + dot_nn(a[0], b[1])


def kernel(chan_ref, basis_ref, ids_ref, hot_ref, hott_ref, coef_ref, flux_ref, begin_ref, turn_ref, vis_ref, flag_ref, kept_ref, sent_ref, ct_ref, cq_ref, jn0_ref, jn1_ref, jt0_ref, jt1_ref, x0h, x0l, x1h, x1l,
           w0h, w0l, w1h, w1l, dp0_ref, dp1_ref, dq0_ref, dq1_ref, acc_ref, pair_ref,
           e0_ref, e1_ref, f0_ref, f1_ref, wide_ref):
    step = pl.program_id(0)
    e_refs, f_refs = (e0_ref, e1_ref), (f0_ref, f1_ref)
    steps = pl.num_programs(0)
    odd = lax.broadcasted_iota(jnp.int32, (32, 128), 1) >= 64
    x_refs = ((x0h, x0l), (x1h, x1l))
    w_refs = ((w0h, w0l), (w1h, w1l))
    jn_refs, jt_refs = (jn0_ref, jn1_ref), (jt0_ref, jt1_ref)
    dp_refs, dq_refs = (dp0_ref, dp1_ref), (dq0_ref, dq1_ref)

    def prepare(slot, chan, before):
        jn_ref, jt_ref = jn_refs[slot], jt_refs[slot]
        element = lax.broadcasted_iota(jnp.int32, (8, 128), 0)
        identity = jnp.where((element == 0) | (element == 6), 1.0, 0.0).astype(f32)
        rows = []
        for k in range(K):
            total = identity
            for b in range(NB):
                total = total + basis_ref[chan, b] * ct_ref[k * 64 + b * 8:k * 64 + b * 8 + 8, :]
            rows.append(total)
        jones = jnp.concatenate(rows + rows, axis=0).T[0:RB]
        halves = [jnp.broadcast_to(ids_ref[0:1, h * 128:(h + 1) * 128], (RB, 128)) for h in range(2)]
        for e in range(8):
            for h in range(2):
                jn_ref[e, :, h * 128:(h + 1) * 128] = jnp.take_along_axis(
                    jones, halves[h] + e, axis=1, mode="promise_in_bounds"
                )
        place = lax.broadcasted_iota(jnp.int32, (K, 512), 1)
        total = jnp.where((place < 64) | ((place >= 320) & (place < 384)), 1.0, 0.0).astype(f32)
        for b in range(NB):
            total = total + basis_ref[chan, b] * cq_ref[b]
        high, low = split(total)
        total = dot_nn(hott_ref[...], jnp.concatenate([high.astype(f32), low.astype(f32)], axis=0).astype(bf16))
        for part in range(4):
            jt_ref[part] = total[:, part * 128:(part + 1) * 128]
        for t in range(T_SMP):
            for side in range(2):
                er, ei = before[0, t, side], before[1, t, side]
                if before is not begin_ref:
                    sr, si = turn_ref[0, t, side], turn_ref[1, t, side]
                    er, ei = er * sr - ei * si, er * si + ei * sr
                e_refs[slot][0, t, side] = er
                e_refs[slot][1, t, side] = ei
            flux = flux_ref[pl.ds(chan, 1), :]
            er, ei = e_refs[slot][0, t, 0] * flux, e_refs[slot][1, t, 0] * flux
            f_refs[slot][0, t] = er
            f_refs[slot][1, t] = ei
            for j in range(2):
                for i in range(2):
                    jr = jn_ref[4 * i + 2 * j]
                    ji = jn_ref[4 * i + 2 * j + 1]
                    for c, value in enumerate((jr * er - ji * ei, jr * ei + ji * er)):
                        spot = slice(c * 128 + i * RB, c * 128 + (i + 1) * RB)
                        for ref, part in zip(x_refs[slot], split(value)):
                            ref[t, spot, j * 256:(j + 1) * 256] = part
            er, ei = e_refs[slot][0, t, 1], e_refs[slot][1, t, 1]
            er = jnp.concatenate([er, er], axis=0).T
            ei = jnp.concatenate([ei, ei], axis=0).T
            for j in range(2):
                jr = jt_ref[2 * j]
                ji = jt_ref[2 * j + 1]
                for c, value in enumerate((jr * er - ji * ei, jr * ei + ji * er)):
                    for ref, part in zip(w_refs[slot], split(value)):
                        ref[t, j * 256:(j + 1) * 256, c * 128:(c + 1) * 128] = part

    def forward(slot, t, row):
        result = product([ref[t] for ref in x_refs[slot]], [ref[t] for ref in w_refs[slot]])
        model = (
            result[0:128, 0:128] + result[128:256, 128:256],
            result[128:256, 0:128] - result[0:128, 128:256],
        )
        resid = []
        for c in range(2):
            observed = []
            for i in range(2):
                one = wide_ref[4 * i + c, t, pl.ds(row, 32, stride=8), :]
                two = wide_ref[4 * i + 2 + c, t, pl.ds(row, 32, stride=8), :]
                observed.append(jnp.where(odd, pltpu.roll(two, 64, 1), one))
                observed.append(jnp.where(odd, two, pltpu.roll(one, 64, 1)))
            resid.append(model[c] - jnp.concatenate(observed, axis=0))
        square = resid[0] * resid[0] + resid[1] * resid[1]
        square = square[0:64] + square[64:128]
        square = square + pltpu.roll(square, 64, 1)
        flag = flag_ref[t, slot].astype(f32) * SCALE
        other = pltpu.roll(flag, 64, 1)
        flag = jnp.concatenate([jnp.where(odd, other, flag), jnp.where(odd, flag, other)], axis=0)
        weight = flag / (2.0 + square)
        weight = jnp.concatenate([weight, weight], axis=0)
        re = (resid[0] * weight).T
        im = (resid[1] * weight).T
        return split(
            jnp.concatenate([jnp.concatenate([re, im], axis=1), jnp.concatenate([-im, re], axis=1)], axis=0)
        )

    def backward(slot, g):
        dp_ref, dq_ref = dp_refs[slot], dq_refs[slot]
        phasors_t = []
        for t in range(T_SMP):
            er, ei = f_refs[slot][0, t], f_refs[slot][1, t]
            phasors_t.append((jnp.concatenate([er, er], axis=0).T, jnp.concatenate([ei, ei], axis=0).T))
        for j in range(2):
            sums = [0.0, 0.0]
            for t in range(T_SMP):
                er, ei = phasors_t[t]
                part = product([ref[t, j * 256:(j + 1) * 256] for ref in w_refs[slot]], g[t])
                dr, di = part[:, 0:128], part[:, 128:256]
                sums = [sums[0] + dr * er + di * ei, sums[1] + di * er - dr * ei]
            for c in range(2):
                dp_ref[:, (2 * j + c) * 128:(2 * j + c + 1) * 128] = sums[c]
        for j in range(2):
            sums = [[0.0, 0.0], [0.0, 0.0]]
            for t in range(T_SMP):
                er, ei = e_refs[slot][0, t, 1], e_refs[slot][1, t, 1]
                part = product(g[t], [ref[t, :, j * 256:(j + 1) * 256] for ref in x_refs[slot]])
                for i in range(2):
                    dr, di = part[i * RB:(i + 1) * RB], part[128 + i * RB:128 + (i + 1) * RB]
                    sums[i] = [sums[i][0] + dr * er + di * ei, sums[i][1] + di * er - dr * ei]
            for i in range(2):
                for c in range(2):
                    e = 4 * i + 2 * j + c
                    dq_ref[e * RB:(e + 1) * RB] = sums[i][c]

    def collect(slot, chan):
        hot = hot_ref[...]
        high, low = split(dp_refs[slot][...])
        sums = [(dot_nn(hot, high) + dot_nn(hot, low))[0:8]]
        high, low = split(dq_refs[slot][...])
        sums.append((dot_nt(hot, high) + dot_nt(hot, low))[0:8])
        for side in range(2):
            for b in range(NB):
                acc_ref[b, side] += basis_ref[chan, b] * sums[side]

    @pl.when(step == 0)
    def _():
        acc_ref[...] = jnp.zeros_like(acc_ref)
        for part in range(4):
            lanes = slice(part * 128, (part + 1) * 128)
            pair_ref[part] = coef_ref[0, :, lanes]
            ct_ref[lanes, :] = jnp.concatenate(
                [
                    pair_ref[part, pl.ds(0, 32, stride=2), :],
                    pair_ref[part, pl.ds(1, 32, stride=2), :],
                    coef_ref[1, :, lanes],
                ],
                axis=0,
            ).T
        for b in range(NB):
            for j in range(2):
                for c in range(2):
                    both = [ct_ref[pl.ds(b * 8 + 4 * i + 2 * j + c, 8, stride=64), :][:, 64:128] for i in range(2)]
                    cq_ref[b, :, (2 * j + c) * 128:(2 * j + c + 1) * 128] = jnp.concatenate(both, axis=1)
        prepare(0, 0, begin_ref)

    first = 2 * step
    row = first // 8 % 2 * 256 + first % 8

    @pl.when(step % 8 == 0)
    def _():
        def widen(index, carry):
            e, t = index // T_SMP, index % T_SMP
            wide = vis_ref[e, t].astype(f32)
            for g in range(2):
                for p in range(32):
                    spot = g * 256 + p * 8
                    wide_ref[e, t, spot:spot + 8, :] = wide[g * 8:(g + 1) * 8, p * 128:(p + 1) * 128]
            return carry

        lax.fori_loop(0, 8 * T_SMP, widen, 0)

    g = [forward(0, t, row) for t in range(T_SMP)]
    prepare(1, first + 1, e0_ref)
    backward(0, g)
    g = [forward(1, t, row + 1) for t in range(T_SMP)]
    prepare(0, jnp.minimum(first + 2, 2 * steps - 1), e1_ref)
    collect(0, first)
    backward(1, g)
    collect(1, first + 1)

    @pl.when(step == steps - 1)
    def _():
        for b in range(NB):
            for e in range(8):
                i, j, c = e // 4, e // 2 % 2, e % 2
                first = (4 * j + 2 * c + i) * RB
                ct_ref[pl.ds(b * 8 + e, 8, stride=64), :] = jnp.concatenate(
                    [acc_ref[b, 0, :, first:first + RB], acc_ref[b, 1, :, e * RB:(e + 1) * RB]], axis=1
                )
        turned = ct_ref[...].T
        first_chan = chan_ref[0] == 0
        for part in range(4):
            lanes = slice(part * 128, (part + 1) * 128)
            pair_ref[part, pl.ds(0, 32, stride=2), :] = turned[0:32, lanes]
            pair_ref[part, pl.ds(1, 32, stride=2), :] = turned[32:64, lanes]
            row_part, col_part = pair_ref[part], turned[64:128, lanes]
            kept_ref[:, lanes] = jnp.where(first_chan, row_part, col_part)
            sent_ref[:, lanes] = jnp.where(first_chan, col_part, row_part)


def gradient_call(chan, basis, ids, hot, coef, flux, begin, turn, vis, flag):
    chans = basis.shape[0]
    const = lambda shape: pl.BlockSpec(shape, lambda f: (0,) * len(shape))
    hott = jnp.concatenate([hot[0:8], hot[0:8]], axis=0).T
    factors = []
    for shape in ((T_SMP, 256, 512), (T_SMP, 512, 256)):
        factors += [pltpu.VMEM(shape, bf16)] * 4
    return pl.pallas_call(
        kernel,
        grid=(chans // 2,),
        in_specs=[
            pl.BlockSpec(memory_space=pltpu.SMEM),
            pl.BlockSpec(memory_space=pltpu.SMEM),
            const((8, NSRC)),
            const((16, NSRC)),
            const((NSRC, 16)),
            const((2, RB, 512)),
            const(flux.shape),
            const(begin.shape),
            const(turn.shape),
            pl.BlockSpec((8, T_SMP, 16, BLK), lambda f: (0, 0, f // 8, 0)),
            pl.BlockSpec((T_SMP, 2, 32, 128), lambda f: (0, f, 0, 0)),
        ],
        out_specs=[const((RB, 512))] * 2,
        out_shape=[jax.ShapeDtypeStruct((RB, 512), f32)] * 2,
        scratch_shapes=[
            pltpu.VMEM((512, 128), f32),
            pltpu.VMEM((NB, K, 512), f32),
            pltpu.VMEM((8, RB, NSRC), f32),
            pltpu.VMEM((8, RB, NSRC), f32),
            pltpu.VMEM((4, NSRC, 128), f32),
            pltpu.VMEM((4, NSRC, 128), f32),
            *factors,
            pltpu.VMEM((NSRC, 512), f32),
            pltpu.VMEM((NSRC, 512), f32),
            pltpu.VMEM((512, NSRC), f32),
            pltpu.VMEM((512, NSRC), f32),
            pltpu.VMEM((NB, 2, K, 512), f32),
            pltpu.VMEM((4, RB, 128), f32),
            *[pltpu.VMEM((2, T_SMP, 2, RB, NSRC), f32)] * 2,
            *[pltpu.VMEM((2, T_SMP, RB, NSRC), f32)] * 2,
            pltpu.VMEM((8, T_SMP, 512, 128), f32),
        ],
        compiler_params=pltpu.CompilerParams(
            dimension_semantics=("arbitrary",), vmem_limit_bytes=60 * 1024 * 1024
        ),
        cost_estimate=pl.CostEstimate(
            flops=2 * 3 * 6 * 128 * 1024 * 256 * T_SMP * chans, bytes_accessed=24 * 1024 * 1024, transcendentals=0
        ),
        name="robust_gradient",
    )(chan, basis, ids, hot, hott, coef, flux, begin, turn, vis, flag)


CROSS = [(r * 8 + c, c * 8 + r) for r in range(8) for c in range(8)]


def merge(held, other, axis, bit):
    upper = (lax.axis_index(axis) & bit) != 0
    return jnp.concatenate([jnp.where(upper, other, held), jnp.where(upper, held, other)], axis=0)


def pairs(target):
    index = lambda r, c, h: (r * 8 + c) * 2 + h
    return [(index(r, c, h), index(*target(r, c, h))) for r in range(8) for c in range(8) for h in range(2)]


def per_device(visibility, flags, coeffs, station_uv, source_lm, source_flux, cluster_ids):
    chans = visibility.shape[2]
    row = lax.axis_index("row")
    col = lax.axis_index("col")
    chan_start = lax.axis_index("chan") * chans
    channels = chan_start + jnp.arange(chans)

    basis = bernstein(channels, NB)
    row_uv = lax.dynamic_slice_in_dim(station_uv, row * RB, RB, 2)
    row_uv = row_uv.reshape(2, T_SMP, 32, 2).transpose(0, 1, 3, 2).reshape(2, T_SMP, RB)
    col_uv = lax.dynamic_slice_in_dim(station_uv, col * RB, RB, 2)
    uv = jnp.stack([row_uv, col_uv], axis=2)
    geo = uv[0][..., None] * source_lm[0] + uv[1][..., None] * source_lm[1]
    begin = jnp.stack(phasors(frequency(chan_start) * geo))
    turn = jnp.stack(phasors((0.5 / F) * geo))
    flux = lax.dynamic_slice_in_dim(source_flux, chan_start, chans, 1).T
    ids = jnp.broadcast_to(cluster_ids[None] * 8, (8, NSRC))
    hot = (cluster_ids[None] == jnp.arange(16)[:, None]).astype(bf16)

    vis = visibility.reshape(8, T_SMP, chans, BLK)
    flag = flags.reshape(T_SMP, chans, 32, 128)

    row_coef = coeffs
    col_coef = lax.ppermute(coeffs, ("row", "col"), CROSS)
    for bit in (1, 2, 4):
        row_coef = merge(row_coef, lax.ppermute(row_coef, "col", [(c, c ^ bit) for c in range(8)]), "col", bit)
        col_coef = merge(col_coef, lax.ppermute(col_coef, "row", [(r, r ^ bit) for r in range(8)]), "row", bit)
    coef = jnp.stack([row_coef, col_coef])

    chan = lax.axis_index("chan")
    kept, sent = gradient_call(chan.reshape(1), basis, ids, hot, coef, flux, begin, turn, vis, flag)
    axes = ("row", "col", "chan")
    held = kept + lax.ppermute(sent, axes, pairs(lambda r, c, h: (r, c, 1 - h)))
    place = jnp.where(chan == 0, col, row)
    for bit in (4, 2, 1):
        half = held.shape[0] // 2
        upper = (place & bit) != 0
        low, high = held[:half], held[half:]
        partner = pairs(lambda r, c, h: (r, c ^ bit, h) if h == 0 else (r ^ bit, c, h))
        held = jnp.where(upper, high, low) + lax.ppermute(jnp.where(upper, low, high), axes, partner)
    other = lax.ppermute(held, axes, pairs(lambda r, c, h: (r, c, 1) if h == 0 else (c, r, 0)))
    crossed = lax.ppermute(held, axes, pairs(lambda r, c, h: (c, r, h)))
    return jnp.where(chan == 0, held + other, other + crossed)


def solution(mesh):
    return jax.shard_map(
        per_device,
        mesh=mesh,
        in_specs=(
            P(None, None, "chan", "row", "col", None),
            P(None, "chan", "row", "col", None),
            P(("row", "col"), None),
            P(),
            P(),
            P(),
            P(),
        ),
        out_specs=P(("row", "col"), None),
        check_vma=False,
    )
```

```python
import math

import jax
import jax.numpy as jnp
from jax import lax
from jax.experimental import pallas as pl
from jax.experimental.pallas import tpu as pltpu
from jax.sharding import PartitionSpec as P

S = 512
K = 8
F = 64
NB = 8
NSRC = 256
T_SMP = 2
RB = 64
BLK = 4096
SCALE = 10.0 / math.sqrt(S * F * T_SMP)

f32 = jnp.float32
bf16 = jnp.bfloat16

SIN_TERMS = [(-1) ** n * math.pi ** (2 * n + 1) / math.factorial(2 * n + 1) for n in range(8)]
COS_TERMS = [(-1) ** n * math.pi ** (2 * n) / math.factorial(2 * n) for n in range(8)]


def bernstein(channel_index, nbasis):
    position = (channel_index.astype(f32) + 0.5) / F
    power = jnp.arange(nbasis).astype(f32)
    binomial = jnp.array([math.comb(nbasis - 1, degree) for degree in range(nbasis)], f32)
    return (
        binomial[None, :]
        * position[:, None] ** power[None, :]
        * (1.0 - position)[:, None] ** (nbasis - 1.0 - power)[None, :]
    )


def frequency(channel_index):
    return 1.0 + 0.5 * (channel_index.astype(f32) + 0.5) / F


def horner(terms, y):
    total = terms[-1]
    for term in terms[-2::-1]:
        total = total * y + term
    return total


def phasors(turns):
    r = turns - jnp.round(turns)
    y = r * r
    half_sin = r * horner(SIN_TERMS, y)
    half_cos = horner(COS_TERMS, y)
    return 1.0 - 2.0 * half_sin * half_sin, -2.0 * half_sin * half_cos


def split(x):
    high = x.astype(bf16)
    return high, (x - high.astype(f32)).astype(bf16)


def dot_nn(a, b):
    return lax.dot_general(a, b, (((1,), (0,)), ((), ())), preferred_element_type=f32)


def dot_nt(a, b):
    return lax.dot_general(a, b, (((1,), (1,)), ((), ())), preferred_element_type=f32)


def product(a, b):
    return dot_nn(a[0], b[0]) + dot_nn(a[1], b[0]) + dot_nn(a[0], b[1])


def kernel(basis_ref, ids_ref, hot_ref, hott_ref, coef_ref, flux_ref, begin_ref, turn_ref, vis_ref, flag_ref, row_ref, col_ref, ct_ref, cq_ref, jn0_ref, jn1_ref, jt0_ref, jt1_ref, x0h, x0l, x1h, x1l,
           w0h, w0l, w1h, w1l, dp0_ref, dp1_ref, dq0_ref, dq1_ref, acc_ref, pair_ref,
           e0_ref, e1_ref, f0_ref, f1_ref, wide_ref):
    step = pl.program_id(0)
    e_refs, f_refs = (e0_ref, e1_ref), (f0_ref, f1_ref)
    steps = pl.num_programs(0)
    odd = lax.broadcasted_iota(jnp.int32, (32, 128), 1) >= 64
    x_refs = ((x0h, x0l), (x1h, x1l))
    w_refs = ((w0h, w0l), (w1h, w1l))
    jn_refs, jt_refs = (jn0_ref, jn1_ref), (jt0_ref, jt1_ref)
    dp_refs, dq_refs = (dp0_ref, dp1_ref), (dq0_ref, dq1_ref)

    def prepare(slot, chan, before):
        jn_ref, jt_ref = jn_refs[slot], jt_refs[slot]
        element = lax.broadcasted_iota(jnp.int32, (8, 128), 0)
        identity = jnp.where((element == 0) | (element == 6), 1.0, 0.0).astype(f32)
        rows = []
        for k in range(K):
            total = identity
            for b in range(NB):
                total = total + basis_ref[chan, b] * ct_ref[k * 64 + b * 8:k * 64 + b * 8 + 8, :]
            rows.append(total)
        jones = jnp.concatenate(rows + rows, axis=0).T[0:RB]
        halves = [jnp.broadcast_to(ids_ref[0:1, h * 128:(h + 1) * 128], (RB, 128)) for h in range(2)]
        for e in range(8):
            for h in range(2):
                jn_ref[e, :, h * 128:(h + 1) * 128] = jnp.take_along_axis(
                    jones, halves[h] + e, axis=1, mode="promise_in_bounds"
                )
        place = lax.broadcasted_iota(jnp.int32, (K, 512), 1)
        total = jnp.where((place < 64) | ((place >= 320) & (place < 384)), 1.0, 0.0).astype(f32)
        for b in range(NB):
            total = total + basis_ref[chan, b] * cq_ref[b]
        high, low = split(total)
        total = dot_nn(hott_ref[...], jnp.concatenate([high.astype(f32), low.astype(f32)], axis=0).astype(bf16))
        for part in range(4):
            jt_ref[part] = total[:, part * 128:(part + 1) * 128]
        for t in range(T_SMP):
            for side in range(2):
                er, ei = before[0, t, side], before[1, t, side]
                if before is not begin_ref:
                    sr, si = turn_ref[0, t, side], turn_ref[1, t, side]
                    er, ei = er * sr - ei * si, er * si + ei * sr
                e_refs[slot][0, t, side] = er
                e_refs[slot][1, t, side] = ei
            flux = flux_ref[pl.ds(chan, 1), :]
            er, ei = e_refs[slot][0, t, 0] * flux, e_refs[slot][1, t, 0] * flux
            f_refs[slot][0, t] = er
            f_refs[slot][1, t] = ei
            for j in range(2):
                for i in range(2):
                    jr = jn_ref[4 * i + 2 * j]
                    ji = jn_ref[4 * i + 2 * j + 1]
                    for c, value in enumerate((jr * er - ji * ei, jr * ei + ji * er)):
                        spot = slice(c * 128 + i * RB, c * 128 + (i + 1) * RB)
                        for ref, part in zip(x_refs[slot], split(value)):
                            ref[t, spot, j * 256:(j + 1) * 256] = part
            er, ei = e_refs[slot][0, t, 1], e_refs[slot][1, t, 1]
            er = jnp.concatenate([er, er], axis=0).T
            ei = jnp.concatenate([ei, ei], axis=0).T
            for j in range(2):
                jr = jt_ref[2 * j]
                ji = jt_ref[2 * j + 1]
                for c, value in enumerate((jr * er - ji * ei, jr * ei + ji * er)):
                    for ref, part in zip(w_refs[slot], split(value)):
                        ref[t, j * 256:(j + 1) * 256, c * 128:(c + 1) * 128] = part

    def forward(slot, t, row):
        result = product([ref[t] for ref in x_refs[slot]], [ref[t] for ref in w_refs[slot]])
        model = (
            result[0:128, 0:128] + result[128:256, 128:256],
            result[128:256, 0:128] - result[0:128, 128:256],
        )
        resid = []
        for c in range(2):
            observed = []
            for i in range(2):
                one = wide_ref[4 * i + c, t, pl.ds(row, 32, stride=8), :]
                two = wide_ref[4 * i + 2 + c, t, pl.ds(row, 32, stride=8), :]
                observed.append(jnp.where(odd, pltpu.roll(two, 64, 1), one))
                observed.append(jnp.where(odd, two, pltpu.roll(one, 64, 1)))
            resid.append(model[c] - jnp.concatenate(observed, axis=0))
        square = resid[0] * resid[0] + resid[1] * resid[1]
        square = square[0:64] + square[64:128]
        square = square + pltpu.roll(square, 64, 1)
        flag = flag_ref[t, slot].astype(f32) * SCALE
        other = pltpu.roll(flag, 64, 1)
        flag = jnp.concatenate([jnp.where(odd, other, flag), jnp.where(odd, flag, other)], axis=0)
        weight = flag / (2.0 + square)
        weight = jnp.concatenate([weight, weight], axis=0)
        re = (resid[0] * weight).T
        im = (resid[1] * weight).T
        return split(
            jnp.concatenate([jnp.concatenate([re, im], axis=1), jnp.concatenate([-im, re], axis=1)], axis=0)
        )

    def backward(slot, g):
        dp_ref, dq_ref = dp_refs[slot], dq_refs[slot]
        phasors_t = []
        for t in range(T_SMP):
            er, ei = f_refs[slot][0, t], f_refs[slot][1, t]
            phasors_t.append((jnp.concatenate([er, er], axis=0).T, jnp.concatenate([ei, ei], axis=0).T))
        for j in range(2):
            sums = [0.0, 0.0]
            for t in range(T_SMP):
                er, ei = phasors_t[t]
                part = product([ref[t, j * 256:(j + 1) * 256] for ref in w_refs[slot]], g[t])
                dr, di = part[:, 0:128], part[:, 128:256]
                sums = [sums[0] + dr * er + di * ei, sums[1] + di * er - dr * ei]
            for c in range(2):
                dp_ref[:, (2 * j + c) * 128:(2 * j + c + 1) * 128] = sums[c]
        for j in range(2):
            sums = [[0.0, 0.0], [0.0, 0.0]]
            for t in range(T_SMP):
                er, ei = e_refs[slot][0, t, 1], e_refs[slot][1, t, 1]
                part = product(g[t], [ref[t, :, j * 256:(j + 1) * 256] for ref in x_refs[slot]])
                for i in range(2):
                    dr, di = part[i * RB:(i + 1) * RB], part[128 + i * RB:128 + (i + 1) * RB]
                    sums[i] = [sums[i][0] + dr * er + di * ei, sums[i][1] + di * er - dr * ei]
            for i in range(2):
                for c in range(2):
                    e = 4 * i + 2 * j + c
                    dq_ref[e * RB:(e + 1) * RB] = sums[i][c]

    def collect(slot, chan):
        hot = hot_ref[...]
        high, low = split(dp_refs[slot][...])
        sums = [(dot_nn(hot, high) + dot_nn(hot, low))[0:8]]
        high, low = split(dq_refs[slot][...])
        sums.append((dot_nt(hot, high) + dot_nt(hot, low))[0:8])
        for side in range(2):
            for b in range(NB):
                acc_ref[b, side] += basis_ref[chan, b] * sums[side]

    @pl.when(step == 0)
    def _():
        acc_ref[...] = jnp.zeros_like(acc_ref)
        for part in range(4):
            lanes = slice(part * 128, (part + 1) * 128)
            pair_ref[part] = coef_ref[0, :, lanes]
            ct_ref[lanes, :] = jnp.concatenate(
                [
                    pair_ref[part, pl.ds(0, 32, stride=2), :],
                    pair_ref[part, pl.ds(1, 32, stride=2), :],
                    coef_ref[1, :, lanes],
                ],
                axis=0,
            ).T
        for b in range(NB):
            for j in range(2):
                for c in range(2):
                    both = [ct_ref[pl.ds(b * 8 + 4 * i + 2 * j + c, 8, stride=64), :][:, 64:128] for i in range(2)]
                    cq_ref[b, :, (2 * j + c) * 128:(2 * j + c + 1) * 128] = jnp.concatenate(both, axis=1)
        prepare(0, 0, begin_ref)

    first = 2 * step
    row = first // 8 % 2 * 256 + first % 8

    @pl.when(step % 8 == 0)
    def _():
        def widen(index, carry):
            e, t = index // T_SMP, index % T_SMP
            wide = vis_ref[e, t].astype(f32)
            for g in range(2):
                for p in range(32):
                    spot = g * 256 + p * 8
                    wide_ref[e, t, spot:spot + 8, :] = wide[g * 8:(g + 1) * 8, p * 128:(p + 1) * 128]
            return carry

        lax.fori_loop(0, 8 * T_SMP, widen, 0)

    g = [forward(0, t, row) for t in range(T_SMP)]
    prepare(1, first + 1, e0_ref)
    backward(0, g)
    g = [forward(1, t, row + 1) for t in range(T_SMP)]
    prepare(0, jnp.minimum(first + 2, 2 * steps - 1), e1_ref)
    collect(0, first)
    backward(1, g)
    collect(1, first + 1)

    @pl.when(step == steps - 1)
    def _():
        for b in range(NB):
            for e in range(8):
                i, j, c = e // 4, e // 2 % 2, e % 2
                first = (4 * j + 2 * c + i) * RB
                ct_ref[pl.ds(b * 8 + e, 8, stride=64), :] = jnp.concatenate(
                    [acc_ref[b, 0, :, first:first + RB], acc_ref[b, 1, :, e * RB:(e + 1) * RB]], axis=1
                )
        turned = ct_ref[...].T
        col_ref[...] = turned[64:128]
        for part in range(4):
            lanes = slice(part * 128, (part + 1) * 128)
            pair_ref[part, pl.ds(0, 32, stride=2), :] = turned[0:32, lanes]
            pair_ref[part, pl.ds(1, 32, stride=2), :] = turned[32:64, lanes]
            row_ref[:, lanes] = pair_ref[part]


def gradient_call(basis, ids, hot, coef, flux, begin, turn, vis, flag):
    chans = basis.shape[0]
    const = lambda shape: pl.BlockSpec(shape, lambda f: (0,) * len(shape))
    hott = jnp.concatenate([hot[0:8], hot[0:8]], axis=0).T
    factors = []
    for shape in ((T_SMP, 256, 512), (T_SMP, 512, 256)):
        factors += [pltpu.VMEM(shape, bf16)] * 4
    return pl.pallas_call(
        kernel,
        grid=(chans // 2,),
        in_specs=[
            pl.BlockSpec(memory_space=pltpu.SMEM),
            const((8, NSRC)),
            const((16, NSRC)),
            const((NSRC, 16)),
            const((2, RB, 512)),
            const(flux.shape),
            const(begin.shape),
            const(turn.shape),
            pl.BlockSpec((8, T_SMP, 16, BLK), lambda f: (0, 0, f // 8, 0)),
            pl.BlockSpec((T_SMP, 2, 32, 128), lambda f: (0, f, 0, 0)),
        ],
        out_specs=[const((RB, 512))] * 2,
        out_shape=[jax.ShapeDtypeStruct((RB, 512), f32)] * 2,
        scratch_shapes=[
            pltpu.VMEM((512, 128), f32),
            pltpu.VMEM((NB, K, 512), f32),
            pltpu.VMEM((8, RB, NSRC), f32),
            pltpu.VMEM((8, RB, NSRC), f32),
            pltpu.VMEM((4, NSRC, 128), f32),
            pltpu.VMEM((4, NSRC, 128), f32),
            *factors,
            pltpu.VMEM((NSRC, 512), f32),
            pltpu.VMEM((NSRC, 512), f32),
            pltpu.VMEM((512, NSRC), f32),
            pltpu.VMEM((512, NSRC), f32),
            pltpu.VMEM((NB, 2, K, 512), f32),
            pltpu.VMEM((4, RB, 128), f32),
            *[pltpu.VMEM((2, T_SMP, 2, RB, NSRC), f32)] * 2,
            *[pltpu.VMEM((2, T_SMP, RB, NSRC), f32)] * 2,
            pltpu.VMEM((8, T_SMP, 512, 128), f32),
        ],
        compiler_params=pltpu.CompilerParams(
            dimension_semantics=("arbitrary",), vmem_limit_bytes=60 * 1024 * 1024
        ),
        cost_estimate=pl.CostEstimate(
            flops=2 * 3 * 6 * 128 * 1024 * 256 * T_SMP * chans, bytes_accessed=24 * 1024 * 1024, transcendentals=0
        ),
        name="robust_gradient",
    )(basis, ids, hot, hott, coef, flux, begin, turn, vis, flag)


CROSS = [(r * 8 + c, c * 8 + r) for r in range(8) for c in range(8)]


def merge(held, other, axis, bit):
    upper = (lax.axis_index(axis) & bit) != 0
    return jnp.concatenate([jnp.where(upper, other, held), jnp.where(upper, held, other)], axis=0)


def per_device(visibility, flags, coeffs, station_uv, source_lm, source_flux, cluster_ids):
    chans = visibility.shape[2]
    row = lax.axis_index("row")
    col = lax.axis_index("col")
    chan_start = lax.axis_index("chan") * chans
    channels = chan_start + jnp.arange(chans)

    flux = lax.dynamic_slice_in_dim(source_flux, chan_start, chans, 1).T
    ids = jnp.broadcast_to(cluster_ids[None] * 8, (8, NSRC))
    hot = (cluster_ids[None] == jnp.arange(16)[:, None]).astype(bf16)

    vis = visibility.reshape(8, T_SMP, chans, BLK)
    flag = flags.reshape(T_SMP, chans, 32, 128)

    row_coef = coeffs
    col_coef = lax.ppermute(coeffs, ("row", "col"), CROSS)
    station_uv, chan_start = lax.optimization_barrier((station_uv, chan_start, col_coef))[:2]
    channels = chan_start + jnp.arange(chans)
    basis = bernstein(channels, NB)
    row_uv = lax.dynamic_slice_in_dim(station_uv, row * RB, RB, 2)
    row_uv = row_uv.reshape(2, T_SMP, 32, 2).transpose(0, 1, 3, 2).reshape(2, T_SMP, RB)
    col_uv = lax.dynamic_slice_in_dim(station_uv, col * RB, RB, 2)
    uv = jnp.stack([row_uv, col_uv], axis=2)
    geo = uv[0][..., None] * source_lm[0] + uv[1][..., None] * source_lm[1]
    begin = jnp.stack(phasors(frequency(chan_start) * geo))
    turn = jnp.stack(phasors((0.5 / F) * geo))
    for bit in (1, 2, 4):
        row_coef = merge(row_coef, lax.ppermute(row_coef, "col", [(c, c ^ bit) for c in range(8)]), "col", bit)
        col_coef = merge(col_coef, lax.ppermute(col_coef, "row", [(r, r ^ bit) for r in range(8)]), "row", bit)
    coef = jnp.stack([row_coef, col_coef])

    row_part, col_part = gradient_call(basis, ids, hot, coef, flux, begin, turn, vis, flag)
    part = row_part + lax.ppermute(col_part, ("row", "col"), CROSS)
    part = jnp.broadcast_to(part.reshape(8, 1, 8, 512), (8, 2, 8, 512)).reshape(16, 8, 512)
    return lax.all_to_all(part, ("col", "chan"), 0, 0, tiled=True).sum(0)


def solution(mesh):
    return jax.shard_map(
        per_device,
        mesh=mesh,
        in_specs=(
            P(None, None, "chan", "row", "col", None),
            P(None, "chan", "row", "col", None),
            P(("row", "col"), None),
            P(),
            P(),
            P(),
            P(),
        ),
        out_specs=P(("row", "col"), None),
        check_vma=False,
    )
```

```python
import math

import jax
import jax.numpy as jnp
from jax import lax
from jax.experimental import pallas as pl
from jax.experimental.pallas import tpu as pltpu
from jax.sharding import PartitionSpec as P

S = 512
K = 8
F = 64
NB = 8
NSRC = 256
T_SMP = 2
RB = 64
BLK = 4096
SCALE = 10.0 / math.sqrt(S * F * T_SMP)

f32 = jnp.float32
bf16 = jnp.bfloat16

SIN_TERMS = [(-1) ** n * math.pi ** (2 * n + 1) / math.factorial(2 * n + 1) for n in range(8)]
COS_TERMS = [(-1) ** n * math.pi ** (2 * n) / math.factorial(2 * n) for n in range(8)]


def bernstein(channel_index, nbasis):
    position = (channel_index.astype(f32) + 0.5) / F
    power = jnp.arange(nbasis).astype(f32)
    binomial = jnp.array([math.comb(nbasis - 1, degree) for degree in range(nbasis)], f32)
    return (
        binomial[None, :]
        * position[:, None] ** power[None, :]
        * (1.0 - position)[:, None] ** (nbasis - 1.0 - power)[None, :]
    )


def frequency(channel_index):
    return 1.0 + 0.5 * (channel_index.astype(f32) + 0.5) / F


def horner(terms, y):
    total = terms[-1]
    for term in terms[-2::-1]:
        total = total * y + term
    return total


def phasors(turns):
    r = turns - jnp.round(turns)
    y = r * r
    half_sin = r * horner(SIN_TERMS, y)
    half_cos = horner(COS_TERMS, y)
    return 1.0 - 2.0 * half_sin * half_sin, -2.0 * half_sin * half_cos


def split(x):
    high = x.astype(bf16)
    return high, (x - high.astype(f32)).astype(bf16)


def dot_nn(a, b):
    return lax.dot_general(a, b, (((1,), (0,)), ((), ())), preferred_element_type=f32)


def dot_nt(a, b):
    return lax.dot_general(a, b, (((1,), (1,)), ((), ())), preferred_element_type=f32)


def product(a, b):
    return dot_nn(a[0], b[0]) + dot_nn(a[1], b[0]) + dot_nn(a[0], b[1])


def kernel(basis_ref, ids_ref, hot_ref, hott_ref, coef_ref, flux_ref, begin_ref, turn_ref, vis_ref, flag_ref, row_ref, col_ref, ct_ref, cq_ref, jn0_ref, jn1_ref, jt0_ref, jt1_ref, x0h, x0l, x1h, x1l,
           w0h, w0l, w1h, w1l, dp0_ref, dp1_ref, dq0_ref, dq1_ref, acc_ref, pair_ref,
           e0_ref, e1_ref, f0_ref, f1_ref, wide_ref):
    step = pl.program_id(0)
    e_refs, f_refs = (e0_ref, e1_ref), (f0_ref, f1_ref)
    steps = pl.num_programs(0)
    odd = lax.broadcasted_iota(jnp.int32, (32, 128), 1) >= 64
    x_refs = ((x0h, x0l), (x1h, x1l))
    w_refs = ((w0h, w0l), (w1h, w1l))
    jn_refs, jt_refs = (jn0_ref, jn1_ref), (jt0_ref, jt1_ref)
    dp_refs, dq_refs = (dp0_ref, dp1_ref), (dq0_ref, dq1_ref)

    def prepare(slot, chan, before):
        jn_ref, jt_ref = jn_refs[slot], jt_refs[slot]
        element = lax.broadcasted_iota(jnp.int32, (8, 128), 0)
        identity = jnp.where((element == 0) | (element == 6), 1.0, 0.0).astype(f32)
        rows = []
        for k in range(K):
            total = identity
            for b in range(NB):
                total = total + basis_ref[chan, b] * ct_ref[k * 64 + b * 8:k * 64 + b * 8 + 8, :]
            rows.append(total)
        jones = jnp.concatenate(rows + rows, axis=0).T[0:RB]
        halves = [jnp.broadcast_to(ids_ref[0:1, h * 128:(h + 1) * 128], (RB, 128)) for h in range(2)]
        for e in range(8):
            for h in range(2):
                jn_ref[e, :, h * 128:(h + 1) * 128] = jnp.take_along_axis(
                    jones, halves[h] + e, axis=1, mode="promise_in_bounds"
                )
        place = lax.broadcasted_iota(jnp.int32, (K, 512), 1)
        total = jnp.where((place < 64) | ((place >= 320) & (place < 384)), 1.0, 0.0).astype(f32)
        for b in range(NB):
            total = total + basis_ref[chan, b] * cq_ref[b]
        high, low = split(total)
        total = dot_nn(hott_ref[...], jnp.concatenate([high.astype(f32), low.astype(f32)], axis=0).astype(bf16))
        for part in range(4):
            jt_ref[part] = total[:, part * 128:(part + 1) * 128]
        for t in range(T_SMP):
            for side in range(2):
                er, ei = before[0, t, side], before[1, t, side]
                if before is not begin_ref:
                    sr, si = turn_ref[0, t, side], turn_ref[1, t, side]
                    er, ei = er * sr - ei * si, er * si + ei * sr
                e_refs[slot][0, t, side] = er
                e_refs[slot][1, t, side] = ei
            flux = flux_ref[pl.ds(chan, 1), :]
            er, ei = e_refs[slot][0, t, 0] * flux, e_refs[slot][1, t, 0] * flux
            f_refs[slot][0, t] = er
            f_refs[slot][1, t] = ei
            for j in range(2):
                for i in range(2):
                    jr = jn_ref[4 * i + 2 * j]
                    ji = jn_ref[4 * i + 2 * j + 1]
                    for c, value in enumerate((jr * er - ji * ei, jr * ei + ji * er)):
                        spot = slice(c * 128 + i * RB, c * 128 + (i + 1) * RB)
                        for ref, part in zip(x_refs[slot], split(value)):
                            ref[t, spot, j * 256:(j + 1) * 256] = part
            er, ei = e_refs[slot][0, t, 1], e_refs[slot][1, t, 1]
            er = jnp.concatenate([er, er], axis=0).T
            ei = jnp.concatenate([ei, ei], axis=0).T
            for j in range(2):
                jr = jt_ref[2 * j]
                ji = jt_ref[2 * j + 1]
                for c, value in enumerate((jr * er - ji * ei, jr * ei + ji * er)):
                    for ref, part in zip(w_refs[slot], split(value)):
                        ref[t, j * 256:(j + 1) * 256, c * 128:(c + 1) * 128] = part

    def forward(slot, t, row):
        result = product([ref[t] for ref in x_refs[slot]], [ref[t] for ref in w_refs[slot]])
        model = (
            result[0:128, 0:128] + result[128:256, 128:256],
            result[128:256, 0:128] - result[0:128, 128:256],
        )
        resid = []
        for c in range(2):
            observed = []
            for i in range(2):
                one = wide_ref[4 * i + c, t, pl.ds(row, 32, stride=8), :]
                two = wide_ref[4 * i + 2 + c, t, pl.ds(row, 32, stride=8), :]
                observed.append(jnp.where(odd, pltpu.roll(two, 64, 1), one))
                observed.append(jnp.where(odd, two, pltpu.roll(one, 64, 1)))
            resid.append(model[c] - jnp.concatenate(observed, axis=0))
        square = resid[0] * resid[0] + resid[1] * resid[1]
        square = square[0:64] + square[64:128]
        square = square + pltpu.roll(square, 64, 1)
        flag = flag_ref[t, slot].astype(f32) * SCALE
        other = pltpu.roll(flag, 64, 1)
        flag = jnp.concatenate([jnp.where(odd, other, flag), jnp.where(odd, flag, other)], axis=0)
        weight = flag / (2.0 + square)
        weight = jnp.concatenate([weight, weight], axis=0)
        re = (resid[0] * weight).T
        im = (resid[1] * weight).T
        return split(
            jnp.concatenate([jnp.concatenate([re, im], axis=1), jnp.concatenate([-im, re], axis=1)], axis=0)
        )

    def backward(slot, g):
        dp_ref, dq_ref = dp_refs[slot], dq_refs[slot]
        phasors_t = []
        for t in range(T_SMP):
            er, ei = f_refs[slot][0, t], f_refs[slot][1, t]
            phasors_t.append((jnp.concatenate([er, er], axis=0).T, jnp.concatenate([ei, ei], axis=0).T))
        for j in range(2):
            sums = [0.0, 0.0]
            for t in range(T_SMP):
                er, ei = phasors_t[t]
                part = product([ref[t, j * 256:(j + 1) * 256] for ref in w_refs[slot]], g[t])
                dr, di = part[:, 0:128], part[:, 128:256]
                sums = [sums[0] + dr * er + di * ei, sums[1] + di * er - dr * ei]
            for c in range(2):
                dp_ref[:, (2 * j + c) * 128:(2 * j + c + 1) * 128] = sums[c]
        for j in range(2):
            sums = [[0.0, 0.0], [0.0, 0.0]]
            for t in range(T_SMP):
                er, ei = e_refs[slot][0, t, 1], e_refs[slot][1, t, 1]
                part = product(g[t], [ref[t, :, j * 256:(j + 1) * 256] for ref in x_refs[slot]])
                for i in range(2):
                    dr, di = part[i * RB:(i + 1) * RB], part[128 + i * RB:128 + (i + 1) * RB]
                    sums[i] = [sums[i][0] + dr * er + di * ei, sums[i][1] + di * er - dr * ei]
            for i in range(2):
                for c in range(2):
                    e = 4 * i + 2 * j + c
                    dq_ref[e * RB:(e + 1) * RB] = sums[i][c]

    def collect(slot, chan):
        hot = hot_ref[...]
        high, low = split(dp_refs[slot][...])
        sums = [(dot_nn(hot, high) + dot_nn(hot, low))[0:8]]
        high, low = split(dq_refs[slot][...])
        sums.append((dot_nt(hot, high) + dot_nt(hot, low))[0:8])
        for side in range(2):
            for b in range(NB):
                acc_ref[b, side] += basis_ref[chan, b] * sums[side]

    @pl.when(step == 0)
    def _():
        acc_ref[...] = jnp.zeros_like(acc_ref)
        for part in range(4):
            lanes = slice(part * 128, (part + 1) * 128)
            pair_ref[part] = coef_ref[0, :, lanes]
            ct_ref[lanes, :] = jnp.concatenate(
                [
                    pair_ref[part, pl.ds(0, 32, stride=2), :],
                    pair_ref[part, pl.ds(1, 32, stride=2), :],
                    coef_ref[1, :, lanes],
                ],
                axis=0,
            ).T
        for b in range(NB):
            for j in range(2):
                for c in range(2):
                    both = [ct_ref[pl.ds(b * 8 + 4 * i + 2 * j + c, 8, stride=64), :][:, 64:128] for i in range(2)]
                    cq_ref[b, :, (2 * j + c) * 128:(2 * j + c + 1) * 128] = jnp.concatenate(both, axis=1)
        prepare(0, 0, begin_ref)

    first = 2 * step
    row = first // 8 % 2 * 256 + first % 8

    @pl.when(step % 8 == 0)
    def _():
        def widen(index, carry):
            e, t = index // T_SMP, index % T_SMP
            wide = vis_ref[e, t].astype(f32)
            for g in range(2):
                for p in range(32):
                    spot = g * 256 + p * 8
                    wide_ref[e, t, spot:spot + 8, :] = wide[g * 8:(g + 1) * 8, p * 128:(p + 1) * 128]
            return carry

        lax.fori_loop(0, 8 * T_SMP, widen, 0)

    g = [forward(0, t, row) for t in range(T_SMP)]
    prepare(1, first + 1, e0_ref)
    backward(0, g)
    g = [forward(1, t, row + 1) for t in range(T_SMP)]
    prepare(0, jnp.minimum(first + 2, 2 * steps - 1), e1_ref)
    collect(0, first)
    backward(1, g)
    collect(1, first + 1)

    @pl.when(step == steps - 1)
    def _():
        for b in range(NB):
            for e in range(8):
                i, j, c = e // 4, e // 2 % 2, e % 2
                first = (4 * j + 2 * c + i) * RB
                ct_ref[pl.ds(b * 8 + e, 8, stride=64), :] = jnp.concatenate(
                    [acc_ref[b, 0, :, first:first + RB], acc_ref[b, 1, :, e * RB:(e + 1) * RB]], axis=1
                )
        turned = ct_ref[...].T
        col_ref[...] = turned[64:128]
        for part in range(4):
            lanes = slice(part * 128, (part + 1) * 128)
            pair_ref[part, pl.ds(0, 32, stride=2), :] = turned[0:32, lanes]
            pair_ref[part, pl.ds(1, 32, stride=2), :] = turned[32:64, lanes]
            row_ref[:, lanes] = pair_ref[part]


def gradient_call(basis, ids, hot, coef, flux, begin, turn, vis, flag):
    chans = basis.shape[0]
    const = lambda shape: pl.BlockSpec(shape, lambda f: (0,) * len(shape))
    hott = jnp.concatenate([hot[0:8], hot[0:8]], axis=0).T
    factors = []
    for shape in ((T_SMP, 256, 512), (T_SMP, 512, 256)):
        factors += [pltpu.VMEM(shape, bf16)] * 4
    return pl.pallas_call(
        kernel,
        grid=(chans // 2,),
        in_specs=[
            pl.BlockSpec(memory_space=pltpu.SMEM),
            const((8, NSRC)),
            const((16, NSRC)),
            const((NSRC, 16)),
            const((2, RB, 512)),
            const(flux.shape),
            const(begin.shape),
            const(turn.shape),
            pl.BlockSpec((8, T_SMP, 16, BLK), lambda f: (0, 0, f // 8, 0)),
            pl.BlockSpec((T_SMP, 2, 32, 128), lambda f: (0, f, 0, 0)),
        ],
        out_specs=[const((RB, 512))] * 2,
        out_shape=[jax.ShapeDtypeStruct((RB, 512), f32)] * 2,
        scratch_shapes=[
            pltpu.VMEM((512, 128), f32),
            pltpu.VMEM((NB, K, 512), f32),
            pltpu.VMEM((8, RB, NSRC), f32),
            pltpu.VMEM((8, RB, NSRC), f32),
            pltpu.VMEM((4, NSRC, 128), f32),
            pltpu.VMEM((4, NSRC, 128), f32),
            *factors,
            pltpu.VMEM((NSRC, 512), f32),
            pltpu.VMEM((NSRC, 512), f32),
            pltpu.VMEM((512, NSRC), f32),
            pltpu.VMEM((512, NSRC), f32),
            pltpu.VMEM((NB, 2, K, 512), f32),
            pltpu.VMEM((4, RB, 128), f32),
            *[pltpu.VMEM((2, T_SMP, 2, RB, NSRC), f32)] * 2,
            *[pltpu.VMEM((2, T_SMP, RB, NSRC), f32)] * 2,
            pltpu.VMEM((8, T_SMP, 512, 128), f32),
        ],
        compiler_params=pltpu.CompilerParams(
            dimension_semantics=("arbitrary",), vmem_limit_bytes=60 * 1024 * 1024
        ),
        cost_estimate=pl.CostEstimate(
            flops=2 * 3 * 6 * 128 * 1024 * 256 * T_SMP * chans, bytes_accessed=24 * 1024 * 1024, transcendentals=0
        ),
        name="robust_gradient",
    )(basis, ids, hot, hott, coef, flux, begin, turn, vis, flag)


CROSS = [(r * 8 + c, c * 8 + r) for r in range(8) for c in range(8)]


def merge(held, other, axis, bit):
    upper = (lax.axis_index(axis) & bit) != 0
    return jnp.concatenate([jnp.where(upper, other, held), jnp.where(upper, held, other)], axis=0)


def per_device(visibility, flags, coeffs, station_uv, source_lm, source_flux, cluster_ids):
    chans = visibility.shape[2]
    row = lax.axis_index("row")
    col = lax.axis_index("col")
    chan_start = lax.axis_index("chan") * chans
    channels = chan_start + jnp.arange(chans)

    flux = lax.dynamic_slice_in_dim(source_flux, chan_start, chans, 1).T
    ids = jnp.broadcast_to(cluster_ids[None] * 8, (8, NSRC))
    hot = (cluster_ids[None] == jnp.arange(16)[:, None]).astype(bf16)

    vis = visibility.reshape(8, T_SMP, chans, BLK)
    flag = flags.reshape(T_SMP, chans, 32, 128)

    row_four = [coeffs] + [lax.ppermute(coeffs, "col", [(c, c ^ m) for c in range(8)]) for m in range(1, 4)]
    col_four = [
        lax.ppermute(coeffs, ("row", "col"), [(a * 8 + b, (b ^ m) * 8 + a) for a in range(8) for b in range(8)])
        for m in range(4)
    ]
    row_coef = merge(merge(*row_four[:2], "col", 1), merge(*row_four[2:], "col", 1), "col", 2)
    col_coef = merge(merge(*col_four[:2], "row", 1), merge(*col_four[2:], "row", 1), "row", 2)
    station_uv, chan_start = lax.optimization_barrier((station_uv, chan_start, row_coef))[:2]
    channels = chan_start + jnp.arange(chans)
    basis = bernstein(channels, NB)
    row_uv = lax.dynamic_slice_in_dim(station_uv, row * RB, RB, 2)
    row_uv = row_uv.reshape(2, T_SMP, 32, 2).transpose(0, 1, 3, 2).reshape(2, T_SMP, RB)
    col_uv = lax.dynamic_slice_in_dim(station_uv, col * RB, RB, 2)
    uv = jnp.stack([row_uv, col_uv], axis=2)
    geo = uv[0][..., None] * source_lm[0] + uv[1][..., None] * source_lm[1]
    begin = jnp.stack(phasors(frequency(chan_start) * geo))
    turn = jnp.stack(phasors((0.5 / F) * geo))
    row_coef = merge(row_coef, lax.ppermute(row_coef, "col", [(c, c ^ 4) for c in range(8)]), "col", 4)
    col_coef = merge(col_coef, lax.ppermute(col_coef, "row", [(r, r ^ 4) for r in range(8)]), "row", 4)
    coef = jnp.stack([row_coef, col_coef])

    row_part, col_part = gradient_call(basis, ids, hot, coef, flux, begin, turn, vis, flag)
    part = row_part + lax.ppermute(col_part, ("row", "col"), CROSS)
    part = jnp.broadcast_to(part.reshape(8, 1, 8, 512), (8, 2, 8, 512)).reshape(16, 8, 512)
    return lax.all_to_all(part, ("col", "chan"), 0, 0, tiled=True).sum(0)


def solution(mesh):
    return jax.shard_map(
        per_device,
        mesh=mesh,
        in_specs=(
            P(None, None, "chan", "row", "col", None),
            P(None, "chan", "row", "col", None),
            P(("row", "col"), None),
            P(),
            P(),
            P(),
            P(),
        ),
        out_specs=P(("row", "col"), None),
        check_vma=False,
    )
```

```python
import math

import jax
import jax.numpy as jnp
from jax import lax
from jax.experimental import pallas as pl
from jax.experimental.pallas import tpu as pltpu
from jax.sharding import PartitionSpec as P

S = 512
K = 8
F = 64
NB = 8
NSRC = 256
T_SMP = 2
RB = 64
BLK = 4096
SCALE = 10.0 / math.sqrt(S * F * T_SMP)

f32 = jnp.float32
bf16 = jnp.bfloat16

SIN_TERMS = [(-1) ** n * math.pi ** (2 * n + 1) / math.factorial(2 * n + 1) for n in range(8)]
COS_TERMS = [(-1) ** n * math.pi ** (2 * n) / math.factorial(2 * n) for n in range(8)]


def bernstein(channel_index, nbasis):
    position = (channel_index.astype(f32) + 0.5) / F
    power = jnp.arange(nbasis).astype(f32)
    binomial = jnp.array([math.comb(nbasis - 1, degree) for degree in range(nbasis)], f32)
    return (
        binomial[None, :]
        * position[:, None] ** power[None, :]
        * (1.0 - position)[:, None] ** (nbasis - 1.0 - power)[None, :]
    )


def frequency(channel_index):
    return 1.0 + 0.5 * (channel_index.astype(f32) + 0.5) / F


def horner(terms, y):
    total = terms[-1]
    for term in terms[-2::-1]:
        total = total * y + term
    return total


def phasors(turns):
    r = turns - jnp.round(turns)
    y = r * r
    half_sin = r * horner(SIN_TERMS, y)
    half_cos = horner(COS_TERMS, y)
    return 1.0 - 2.0 * half_sin * half_sin, -2.0 * half_sin * half_cos


def split(x):
    high = x.astype(bf16)
    return high, (x - high.astype(f32)).astype(bf16)


def dot_nn(a, b):
    return lax.dot_general(a, b, (((1,), (0,)), ((), ())), preferred_element_type=f32)


def dot_nt(a, b):
    return lax.dot_general(a, b, (((1,), (1,)), ((), ())), preferred_element_type=f32)


def product(a, b):
    return dot_nn(a[0], b[0]) + dot_nn(a[1], b[0]) + dot_nn(a[0], b[1])


def kernel(basis_ref, ids_ref, hot_ref, hott_ref, coef_ref, flux_ref, begin_ref, turn_ref, vis_ref, flag_ref, row_ref, col_ref, ct_ref, cq_ref, jn0_ref, jn1_ref, jt0_ref, jt1_ref, x0h, x0l, x1h, x1l,
           w0h, w0l, w1h, w1l, dp0_ref, dp1_ref, dq0_ref, dq1_ref, acc_ref, pair_ref,
           e0_ref, e1_ref, f0_ref, f1_ref, wide_ref):
    step = pl.program_id(0)
    e_refs, f_refs = (e0_ref, e1_ref), (f0_ref, f1_ref)
    steps = pl.num_programs(0)
    odd = lax.broadcasted_iota(jnp.int32, (32, 128), 1) >= 64
    x_refs = ((x0h, x0l), (x1h, x1l))
    w_refs = ((w0h, w0l), (w1h, w1l))
    jn_refs, jt_refs = (jn0_ref, jn1_ref), (jt0_ref, jt1_ref)
    dp_refs, dq_refs = (dp0_ref, dp1_ref), (dq0_ref, dq1_ref)

    def prepare(slot, chan, before):
        jn_ref, jt_ref = jn_refs[slot], jt_refs[slot]
        element = lax.broadcasted_iota(jnp.int32, (8, 128), 0)
        identity = jnp.where((element == 0) | (element == 6), 1.0, 0.0).astype(f32)
        rows = []
        for k in range(K):
            total = identity
            for b in range(NB):
                total = total + basis_ref[chan, b] * ct_ref[k * 64 + b * 8:k * 64 + b * 8 + 8, :]
            rows.append(total)
        jones = jnp.concatenate(rows + rows, axis=0).T[0:RB]
        halves = [jnp.broadcast_to(ids_ref[0:1, h * 128:(h + 1) * 128], (RB, 128)) for h in range(2)]
        for e in range(8):
            for h in range(2):
                jn_ref[e, :, h * 128:(h + 1) * 128] = jnp.take_along_axis(
                    jones, halves[h] + e, axis=1, mode="promise_in_bounds"
                )
        place = lax.broadcasted_iota(jnp.int32, (K, 512), 1)
        total = jnp.where((place < 64) | ((place >= 320) & (place < 384)), 1.0, 0.0).astype(f32)
        for b in range(NB):
            total = total + basis_ref[chan, b] * cq_ref[b]
        high, low = split(total)
        total = dot_nn(hott_ref[...], jnp.concatenate([high.astype(f32), low.astype(f32)], axis=0).astype(bf16))
        for part in range(4):
            jt_ref[part] = total[:, part * 128:(part + 1) * 128]
        for t in range(T_SMP):
            for side in range(2):
                er, ei = before[0, t, side], before[1, t, side]
                if before is not begin_ref:
                    sr, si = turn_ref[0, t, side], turn_ref[1, t, side]
                    er, ei = er * sr - ei * si, er * si + ei * sr
                e_refs[slot][0, t, side] = er
                e_refs[slot][1, t, side] = ei
            flux = flux_ref[pl.ds(chan, 1), :]
            er, ei = e_refs[slot][0, t, 0] * flux, e_refs[slot][1, t, 0] * flux
            f_refs[slot][0, t] = er
            f_refs[slot][1, t] = ei
            for j in range(2):
                for i in range(2):
                    jr = jn_ref[4 * i + 2 * j]
                    ji = jn_ref[4 * i + 2 * j + 1]
                    for c, value in enumerate((jr * er - ji * ei, jr * ei + ji * er)):
                        spot = slice(c * 128 + i * RB, c * 128 + (i + 1) * RB)
                        for ref, part in zip(x_refs[slot], split(value)):
                            ref[t, spot, j * 256:(j + 1) * 256] = part
            er, ei = e_refs[slot][0, t, 1], e_refs[slot][1, t, 1]
            er = jnp.concatenate([er, er], axis=0).T
            ei = jnp.concatenate([ei, ei], axis=0).T
            for j in range(2):
                jr = jt_ref[2 * j]
                ji = jt_ref[2 * j + 1]
                for c, value in enumerate((jr * er - ji * ei, jr * ei + ji * er)):
                    for ref, part in zip(w_refs[slot], split(value)):
                        ref[t, j * 256:(j + 1) * 256, c * 128:(c + 1) * 128] = part

    def forward(slot, t, row):
        result = product([ref[t] for ref in x_refs[slot]], [ref[t] for ref in w_refs[slot]])
        model = (
            result[0:128, 0:128] + result[128:256, 128:256],
            result[128:256, 0:128] - result[0:128, 128:256],
        )
        resid = []
        for c in range(2):
            observed = []
            for i in range(2):
                one = wide_ref[4 * i + c, t, pl.ds(row, 32, stride=8), :]
                two = wide_ref[4 * i + 2 + c, t, pl.ds(row, 32, stride=8), :]
                observed.append(jnp.where(odd, pltpu.roll(two, 64, 1), one))
                observed.append(jnp.where(odd, two, pltpu.roll(one, 64, 1)))
            resid.append(model[c] - jnp.concatenate(observed, axis=0))
        square = resid[0] * resid[0] + resid[1] * resid[1]
        square = square[0:64] + square[64:128]
        square = square + pltpu.roll(square, 64, 1)
        flag = flag_ref[t, slot].astype(f32) * SCALE
        other = pltpu.roll(flag, 64, 1)
        flag = jnp.concatenate([jnp.where(odd, other, flag), jnp.where(odd, flag, other)], axis=0)
        weight = flag / (2.0 + square)
        weight = jnp.concatenate([weight, weight], axis=0)
        re = (resid[0] * weight).T
        im = (resid[1] * weight).T
        return split(
            jnp.concatenate([jnp.concatenate([re, im], axis=1), jnp.concatenate([-im, re], axis=1)], axis=0)
        )

    def backward(slot, g):
        dp_ref, dq_ref = dp_refs[slot], dq_refs[slot]
        phasors_t = []
        for t in range(T_SMP):
            er, ei = f_refs[slot][0, t], f_refs[slot][1, t]
            phasors_t.append((jnp.concatenate([er, er], axis=0).T, jnp.concatenate([ei, ei], axis=0).T))
        for j in range(2):
            sums = [0.0, 0.0]
            for t in range(T_SMP):
                er, ei = phasors_t[t]
                part = product([ref[t, j * 256:(j + 1) * 256] for ref in w_refs[slot]], g[t])
                dr, di = part[:, 0:128], part[:, 128:256]
                sums = [sums[0] + dr * er + di * ei, sums[1] + di * er - dr * ei]
            for c in range(2):
                dp_ref[:, (2 * j + c) * 128:(2 * j + c + 1) * 128] = sums[c]
        for j in range(2):
            sums = [[0.0, 0.0], [0.0, 0.0]]
            for t in range(T_SMP):
                er, ei = e_refs[slot][0, t, 1], e_refs[slot][1, t, 1]
                part = product(g[t], [ref[t, :, j * 256:(j + 1) * 256] for ref in x_refs[slot]])
                for i in range(2):
                    dr, di = part[i * RB:(i + 1) * RB], part[128 + i * RB:128 + (i + 1) * RB]
                    sums[i] = [sums[i][0] + dr * er + di * ei, sums[i][1] + di * er - dr * ei]
            for i in range(2):
                for c in range(2):
                    e = 4 * i + 2 * j + c
                    dq_ref[e * RB:(e + 1) * RB] = sums[i][c]

    def collect(slot, chan):
        hot = hot_ref[...]
        high, low = split(dp_refs[slot][...])
        sums = [(dot_nn(hot, high) + dot_nn(hot, low))[0:8]]
        high, low = split(dq_refs[slot][...])
        sums.append((dot_nt(hot, high) + dot_nt(hot, low))[0:8])
        for side in range(2):
            for b in range(NB):
                acc_ref[b, side] += basis_ref[chan, b] * sums[side]

    @pl.when(step == 0)
    def _():
        acc_ref[...] = jnp.zeros_like(acc_ref)
        for part in range(4):
            lanes = slice(part * 128, (part + 1) * 128)
            pair_ref[part] = coef_ref[0, :, lanes]
            ct_ref[lanes, :] = jnp.concatenate(
                [
                    pair_ref[part, pl.ds(0, 32, stride=2), :],
                    pair_ref[part, pl.ds(1, 32, stride=2), :],
                    coef_ref[1, :, lanes],
                ],
                axis=0,
            ).T
        for b in range(NB):
            for j in range(2):
                for c in range(2):
                    both = [ct_ref[pl.ds(b * 8 + 4 * i + 2 * j + c, 8, stride=64), :][:, 64:128] for i in range(2)]
                    cq_ref[b, :, (2 * j + c) * 128:(2 * j + c + 1) * 128] = jnp.concatenate(both, axis=1)
        prepare(0, 0, begin_ref)

    first = 2 * step
    row = first // 8 % 2 * 256 + first % 8

    @pl.when(step % 8 == 0)
    def _():
        def widen(index, carry):
            e, t = index // T_SMP, index % T_SMP
            wide = vis_ref[e, t].astype(f32)
            for g in range(2):
                for p in range(32):
                    spot = g * 256 + p * 8
                    wide_ref[e, t, spot:spot + 8, :] = wide[g * 8:(g + 1) * 8, p * 128:(p + 1) * 128]
            return carry

        lax.fori_loop(0, 8 * T_SMP, widen, 0)

    g = [forward(0, t, row) for t in range(T_SMP)]
    prepare(1, first + 1, e0_ref)
    backward(0, g)
    g = [forward(1, t, row + 1) for t in range(T_SMP)]
    prepare(0, jnp.minimum(first + 2, 2 * steps - 1), e1_ref)
    collect(0, first)
    backward(1, g)
    collect(1, first + 1)

    @pl.when(step == steps - 1)
    def _():
        for b in range(NB):
            for e in range(8):
                i, j, c = e // 4, e // 2 % 2, e % 2
                first = (4 * j + 2 * c + i) * RB
                ct_ref[pl.ds(b * 8 + e, 8, stride=64), :] = jnp.concatenate(
                    [acc_ref[b, 0, :, first:first + RB], acc_ref[b, 1, :, e * RB:(e + 1) * RB]], axis=1
                )
        turned = ct_ref[...].T
        col_ref[...] = turned[64:128]
        for part in range(4):
            lanes = slice(part * 128, (part + 1) * 128)
            pair_ref[part, pl.ds(0, 32, stride=2), :] = turned[0:32, lanes]
            pair_ref[part, pl.ds(1, 32, stride=2), :] = turned[32:64, lanes]
            row_ref[:, lanes] = pair_ref[part]


def gradient_call(basis, ids, hot, coef, flux, begin, turn, vis, flag):
    chans = basis.shape[0]
    const = lambda shape: pl.BlockSpec(shape, lambda f: (0,) * len(shape))
    hott = jnp.concatenate([hot[0:8], hot[0:8]], axis=0).T
    factors = []
    for shape in ((T_SMP, 256, 512), (T_SMP, 512, 256)):
        factors += [pltpu.VMEM(shape, bf16)] * 4
    return pl.pallas_call(
        kernel,
        grid=(chans // 2,),
        in_specs=[
            pl.BlockSpec(memory_space=pltpu.SMEM),
            const((8, NSRC)),
            const((16, NSRC)),
            const((NSRC, 16)),
            const((2, RB, 512)),
            const(flux.shape),
            const(begin.shape),
            const(turn.shape),
            pl.BlockSpec((8, T_SMP, 16, BLK), lambda f: (0, 0, f // 8, 0)),
            pl.BlockSpec((T_SMP, 2, 32, 128), lambda f: (0, f, 0, 0)),
        ],
        out_specs=[const((RB, 512))] * 2,
        out_shape=[jax.ShapeDtypeStruct((RB, 512), f32)] * 2,
        scratch_shapes=[
            pltpu.VMEM((512, 128), f32),
            pltpu.VMEM((NB, K, 512), f32),
            pltpu.VMEM((8, RB, NSRC), f32),
            pltpu.VMEM((8, RB, NSRC), f32),
            pltpu.VMEM((4, NSRC, 128), f32),
            pltpu.VMEM((4, NSRC, 128), f32),
            *factors,
            pltpu.VMEM((NSRC, 512), f32),
            pltpu.VMEM((NSRC, 512), f32),
            pltpu.VMEM((512, NSRC), f32),
            pltpu.VMEM((512, NSRC), f32),
            pltpu.VMEM((NB, 2, K, 512), f32),
            pltpu.VMEM((4, RB, 128), f32),
            *[pltpu.VMEM((2, T_SMP, 2, RB, NSRC), f32)] * 2,
            *[pltpu.VMEM((2, T_SMP, RB, NSRC), f32)] * 2,
            pltpu.VMEM((8, T_SMP, 512, 128), f32),
        ],
        compiler_params=pltpu.CompilerParams(
            dimension_semantics=("arbitrary",), vmem_limit_bytes=60 * 1024 * 1024
        ),
        cost_estimate=pl.CostEstimate(
            flops=2 * 3 * 6 * 128 * 1024 * 256 * T_SMP * chans, bytes_accessed=24 * 1024 * 1024, transcendentals=0
        ),
        name="robust_gradient",
    )(basis, ids, hot, hott, coef, flux, begin, turn, vis, flag)


CROSS = [(r * 8 + c, c * 8 + r) for r in range(8) for c in range(8)]


def merge(held, other, axis, bit):
    upper = (lax.axis_index(axis) & bit) != 0
    return jnp.concatenate([jnp.where(upper, other, held), jnp.where(upper, held, other)], axis=0)


def per_device(visibility, flags, coeffs, station_uv, source_lm, source_flux, cluster_ids):
    chans = visibility.shape[2]
    row = lax.axis_index("row")
    col = lax.axis_index("col")
    chan_start = lax.axis_index("chan") * chans
    channels = chan_start + jnp.arange(chans)

    flux = lax.dynamic_slice_in_dim(source_flux, chan_start, chans, 1).T
    ids = jnp.broadcast_to(cluster_ids[None] * 8, (8, NSRC))
    hot = (cluster_ids[None] == jnp.arange(16)[:, None]).astype(bf16)

    vis = visibility.reshape(8, T_SMP, chans, BLK)
    flag = flags.reshape(T_SMP, chans, 32, 128)

    row_coef = coeffs
    col_coef = lax.ppermute(coeffs, ("row", "col"), CROSS)
    station_uv, chan_start = lax.optimization_barrier((station_uv, chan_start, col_coef))[:2]
    channels = chan_start + jnp.arange(chans)
    basis = bernstein(channels, NB)
    row_uv = lax.dynamic_slice_in_dim(station_uv, row * RB, RB, 2)
    row_uv = row_uv.reshape(2, T_SMP, 32, 2).transpose(0, 1, 3, 2).reshape(2, T_SMP, RB)
    col_uv = lax.dynamic_slice_in_dim(station_uv, col * RB, RB, 2)
    uv = jnp.stack([row_uv, col_uv], axis=2)
    geo = uv[0][..., None] * source_lm[0] + uv[1][..., None] * source_lm[1]
    begin = jnp.stack(phasors(frequency(chan_start) * geo))
    turn = jnp.stack(phasors((0.5 / F) * geo))
    for bit in (1, 2, 4):
        row_coef = merge(row_coef, lax.ppermute(row_coef, "col", [(c, c ^ bit) for c in range(8)]), "col", bit)
        col_coef = merge(col_coef, lax.ppermute(col_coef, "row", [(r, r ^ bit) for r in range(8)]), "row", bit)
    coef = jnp.stack([row_coef, col_coef])

    row_part, col_part = gradient_call(basis, ids, hot, coef, flux, begin, turn, vis, flag)
    part = row_part + lax.ppermute(col_part, ("row", "col"), CROSS)
    total = lax.all_to_all(part, "col", 0, 0, tiled=True).reshape(8, 8, 512).sum(0)
    return total + lax.ppermute(total, "chan", [(0, 1), (1, 0)])


def solution(mesh):
    return jax.shard_map(
        per_device,
        mesh=mesh,
        in_specs=(
            P(None, None, "chan", "row", "col", None),
            P(None, "chan", "row", "col", None),
            P(("row", "col"), None),
            P(),
            P(),
            P(),
            P(),
        ),
        out_specs=P(("row", "col"), None),
        check_vma=False,
    )
```
